32 devices in a mesh: tm: 4 (over y, x), dp: 8 (over z, core).
Axes of the slice: x: 2, y: 2, z: 4, core: 2. Of those that a mesh axis runs over, the one named last changes fastest.
Arguments:
- history: bfloat16 [8, 8192, 256], P('dp', 'tm'), may hold values from -6 to 6
- now_weight: bfloat16 [256, 1024], replicated, may hold values from -0.25 to 0.25
- past_weight: bfloat16 [256, 1024], replicated, may hold values from -0.25 to 0.25
- gate_bias: float32 [1024], replicated, may hold values from -1 to 1
- residual_weight: bfloat16 [512, 256], replicated, may hold values from -0.25 to 0.25
- skip_weight: bfloat16 [512, 256], replicated, may hold values from -0.25 to 0.25
- out_cotangent: bfloat16 [8, 8192, 256], P('dp', 'tm'), may hold values from -6 to 6
- skip_cotangent: bfloat16 [8, 8192, 256], P('dp', 'tm'), may hold values from -6 to 6
Outputs:
- residual_out: bfloat16 [8, 8192, 256], P('dp', 'tm')
- skip_out: bfloat16 [8, 8192, 256], P('dp', 'tm')
- grad_input: bfloat16 [8, 8192, 256], P('dp', 'tm')
- grad_now: float32 [256, 1024], P('dp')
- grad_past: float32 [256, 1024], P('dp')
- grad_bias: float32 [1024], P('dp')
- grad_residual: float32 [512, 256], P('dp')
- skip_grad: float32 [512, 256], P('dp')
The draws below stay inside these ranges and needn't reach their ends.
All inputs are finite; a program needn't handle non-finite values.
Results may differ from the reference program's by a relative error of at most 0.0048.
Values may be sent and summed in bfloat16 or wider, within the bound.
A program may use at most 64 MiB of HBM per device.

```python
import jax
import jax.numpy as jnp
from jax import lax

RESIDUAL_WIDTH = 256
G = 512
DILATION_STEPS = 2048
B = 8
HISTORY_STEPS = 8192


def strengthened(values, own_key, source, target, blocks, factor):
    owner, partner = [(jnp.arange(values.shape[axis_at]) // (values.shape[axis_at] // blocks)).reshape([-1 if axis == axis_at else 1 for axis in range(values.ndim)]) for axis_at in (source, target)]
    chosen = jax.random.permutation(own_key, blocks)[partner]
    strong = (owner == chosen) | (owner == (partner + blocks // 2) % blocks)
    return jnp.where(strong, factor * values, values)


def block_scale(key, shape, split, smallest, top_value):
    def one(position, parts):
        draws = jax.random.uniform(jax.random.fold_in(jax.random.fold_in(key, 6), position), (parts,), jnp.float32, smallest / len(split), top_value / len(split))
        return jnp.repeat(jnp.exp(draws), shape[position] // parts).reshape((-1,) + (1,) * (len(shape) - position - 1))

    factor_of = one(*split[0])
    for cut in split[1:]:
        factor_of = factor_of * one(*cut)
    return factor_of


def gaussian(stream_key, shape, scale, limit, shards=(), kind=jnp.bfloat16):
    values = jax.random.normal(stream_key, shape, jnp.float32) * scale
    if len(shards) > 0:
        values = block_scale(stream_key, shape, shards, -0.22, 0.18) * values
    return jnp.clip(values, min=-limit, max=limit).astype(kind)


def noise_with(rng, dims, deviation, bound, pieces, heavy, kind=jnp.bfloat16):
    entries = deviation * jax.random.normal(rng, dims, jnp.float32)
    if pieces:
        entries = entries * block_scale(rng, dims, pieces, -0.22, 0.18)
    return jnp.clip(strengthened(entries, jax.random.fold_in(rng, 3), *heavy), -bound, bound).astype(kind)


def setup_inputs(seed: int = 0) -> dict:
    seeds = jax.random.split(jax.random.key(seed), 9)
    history = noise_with(seeds[0], (B, HISTORY_STEPS, RESIDUAL_WIDTH), 1.0, 6.0, ((0, 8), (1, 4)), (0, 2, 8, 2.0))
    now_weight = gaussian(seeds[1], (RESIDUAL_WIDTH, 2 * G), (2 * RESIDUAL_WIDTH) ** -0.5, 0.25)
    past_weight = gaussian(seeds[2], (RESIDUAL_WIDTH, 2 * G), (2 * RESIDUAL_WIDTH) ** -0.5, 0.25)
    gate_bias = jnp.clip(jax.random.uniform(seeds[3], (2 * G,), jnp.float32, -1.0, 1.0), -1.0, 1.0)
    residual_weight = gaussian(seeds[4], (G, RESIDUAL_WIDTH), G ** -0.5, 0.25)
    skip_weight = gaussian(seeds[5], (G, RESIDUAL_WIDTH), G ** -0.5, 0.25)
    out_cotangent = gaussian(seeds[6], (B, HISTORY_STEPS, RESIDUAL_WIDTH), 1.0, 6.0, ((0, 8), (1, 4)))
    skip_cotangent = gaussian(seeds[7], (B, HISTORY_STEPS, RESIDUAL_WIDTH), 1.0, 6.0, ((0, 8), (1, 4)))
    return dict(history=history, now_weight=now_weight, past_weight=past_weight, gate_bias=gate_bias, residual_weight=residual_weight, skip_weight=skip_weight, out_cotangent=out_cotangent, skip_cotangent=skip_cotangent)


def contract_rows(left, right):
    return lax.dot_general(left, right, (((0,), (0,)), ((), ())), preferred_element_type=jnp.float32)


def reference(history, now_weight, past_weight, gate_bias, residual_weight, skip_weight, out_cotangent, skip_cotangent):
    def one_history(carry, item):
        power_series, out_cot, skip_cot = item
        padding_rows = jnp.zeros((DILATION_STEPS, RESIDUAL_WIDTH), power_series.dtype)
        lagged_input = jnp.concatenate([padding_rows, power_series[:HISTORY_STEPS - DILATION_STEPS]], axis=0)
        zeta = jnp.dot(power_series, now_weight, preferred_element_type=jnp.float32)
        zeta = zeta + jnp.dot(lagged_input, past_weight, preferred_element_type=jnp.float32) + gate_bias
        tanh_part = jnp.tanh(zeta[:, :G])
        sigm_part = jax.nn.sigmoid(zeta[:, G:])
        gated = (tanh_part * sigm_part).astype(jnp.bfloat16)
        resid = (power_series.astype(jnp.float32) + jnp.dot(gated, residual_weight, preferred_element_type=jnp.float32)).astype(jnp.bfloat16)
        skipped = jnp.dot(gated, skip_weight, preferred_element_type=jnp.float32).astype(jnp.bfloat16)
        dgated = jnp.dot(out_cot, residual_weight.T, preferred_element_type=jnp.float32)
        dgated = dgated + jnp.dot(skip_cot, skip_weight.T, preferred_element_type=jnp.float32)
        dzeta = jnp.concatenate([dgated * sigm_part * (1.0 - tanh_part * tanh_part),
                                 dgated * tanh_part * sigm_part * (1.0 - sigm_part)], axis=1).astype(jnp.bfloat16)
        reverse_pass = jnp.dot(dzeta, past_weight.T, preferred_element_type=jnp.float32).astype(jnp.bfloat16)
        shifted_rows = jnp.concatenate([reverse_pass[DILATION_STEPS:], jnp.zeros((DILATION_STEPS, RESIDUAL_WIDTH), jnp.bfloat16)], axis=0)
        shifted_rows = lax.optimization_barrier(shifted_rows).astype(jnp.float32)
        grad_in = out_cot.astype(jnp.float32) + jnp.dot(dzeta, now_weight.T, preferred_element_type=jnp.float32) + shifted_rows
        grad_in = grad_in.astype(jnp.bfloat16)
        g_now, g_past, g_bias, g_res, g_skip = carry
        g_now = g_now + contract_rows(power_series, dzeta)
        g_past = g_past + contract_rows(lagged_input, dzeta)
        g_bias = g_bias + jnp.sum(dzeta.astype(jnp.float32), axis=0)
        g_res = g_res + contract_rows(gated, out_cot)
        g_skip = g_skip + contract_rows(gated, skip_cot)
        return (g_now, g_past, g_bias, g_res, g_skip), (resid, skipped, grad_in)

    start = (jnp.zeros((RESIDUAL_WIDTH, 2 * G), jnp.float32), jnp.zeros((RESIDUAL_WIDTH, 2 * G), jnp.float32),
             jnp.zeros((2 * G,), jnp.float32), jnp.zeros((G, RESIDUAL_WIDTH), jnp.float32), jnp.zeros((G, RESIDUAL_WIDTH), jnp.float32))
    sums, outputs = lax.scan(one_history, start, (history, out_cotangent, skip_cotangent))
    return (outputs[0], outputs[1], outputs[2], sums[0], sums[1], sums[2], sums[3], sums[4])
```

```python
import functools

import jax
import jax.numpy as jnp
from jax import lax
from jax.experimental import pallas as pl
from jax.experimental.pallas import tpu as pltpu
from jax.sharding import PartitionSpec as P

DILATION_STEPS = 2048
CHUNK = 512
BIAS_ROWS = 16
F32 = jnp.float32
BF16 = jnp.bfloat16
MESH = pl.DeviceIdType.MESH


def dot(a, b, dims=((1,), (0,))):
    return lax.dot_general(a, b, (dims, ((), ())), preferred_element_type=F32)


NT = ((1,), (1,))
TN = ((0,), (0,))


def layer_kernel(
    T, D,
    hist, now_w, past_w, bias, res_w, skip_w, ocot, scot,
    resid, skipped, grad_in, g_now, g_past, g_bias, g_res, g_skip,
    delayed, bw_send, bw_recv, gi_part, zn, dgs, acc_np, acc_rs, acc_b,
    a_send, a_recv, b_own, b_send, b_recv, tot, c_send, c_recv, d_buf,
    f_ss, f_rs, w_ss, w_rs, a_ss, a_rs, b_ss, b_rs, c_ss, c_rs, d_ss, d_rs,
):
    rows, C = hist.shape
    G = res_w.shape[0]
    H = D // 2
    K = rows // CHUNK
    me = lax.axis_index("tm")
    dp = lax.axis_index("dp")
    par = lax.rem(dp, 2)
    j0 = dp // 2
    up = lax.rem(me + 1, T)
    down = lax.rem(me + T - 1, T)
    has_prev = me > 0
    has_next = me < T - 1
    Rn = C // D
    Rg = G // D
    hg = Rg // 2
    W = 2 * G
    bw = W // D
    lane = W // T

    barrier = pltpu.get_barrier_semaphore()
    for o in range(1, T):
        pl.semaphore_signal(barrier, inc=1, device_id={"tm": lax.rem(me + o, T)}, device_id_type=MESH)
    for o in range(1, H):
        pl.semaphore_signal(
            barrier, inc=1, device_id={"dp": 2 * lax.rem(j0 + o, H) + par}, device_id_type=MESH
        )
    pl.semaphore_signal(barrier, inc=1, device_id={"dp": 2 * j0 + 1 - par}, device_id_type=MESH)
    pl.semaphore_wait(barrier, T - 1 + H)

    def remote(src, dst, ss, rs, target):
        return pltpu.make_async_remote_copy(
            src_ref=src, dst_ref=dst, send_sem=ss, recv_sem=rs, device_id=target, device_id_type=MESH
        )

    def fwd(c):
        s = pl.ds(pl.multiple_of(c * CHUNK, CHUNK), CHUNK)
        return remote(hist.at[s], delayed.at[s], f_ss.at[c], f_rs.at[c], {"tm": up})

    def bwd(c):
        s = pl.ds(pl.multiple_of(c * CHUNK, CHUNK), CHUNK)
        return remote(bw_send.at[s], bw_recv.at[s], w_ss.at[c], w_rs.at[c], {"tm": down})

    @pl.when(has_next)
    def _():
        for c in range(K):
            fwd(c).start()

    @pl.when(me == 0)
    def _():
        delayed[...] = jnp.zeros_like(delayed)

    @pl.when(me == T - 1)
    def _():
        bw_recv[...] = jnp.zeros_like(bw_recv)

    acc_np[...] = jnp.zeros_like(acc_np)
    acc_rs[...] = jnp.zeros_like(acc_rs)
    acc_b[...] = jnp.zeros_like(acc_b)

    def step(c, carry):
        s = pl.ds(pl.multiple_of(c * CHUNK, CHUNK), CHUNK)
        oc = ocot[s, :]
        sc = scot[s, :]
        zn[...] = dot(hist[s, :], now_w[...]) + bias[...]
        dgs[...] = dot(oc, res_w[...], NT) + dot(sc, skip_w[...], NT)

        @pl.when(has_prev)
        def _():
            fwd(c).wait_recv()

        z = zn[...] + dot(delayed[s, :], past_w[...])
        th = jnp.tanh(z[:, :G])
        sg = 0.5 * jnp.tanh(0.5 * z[:, G:]) + 0.5
        ts = th * sg
        gated = ts.astype(BF16)
        dg = dgs[...]
        dza = (dg * sg * (1.0 - th * th)).astype(BF16)
        dzb = (dg * ts * (1.0 - sg)).astype(BF16)
        dz = jnp.concatenate([dza, dzb], axis=1)
        bw_send[s, :] = dot(dz, past_w[...], NT).astype(BF16)

        @pl.when(has_prev)
        def _():
            bwd(c).start()

        acc_np[0:C, :] += dot(hist[s, :], dz, TN)
        acc_np[C:, :] += dot(delayed[s, :], dz, TN)
        acc_rs[:, 0:C] += dot(gated, oc, TN)
        acc_rs[:, C:] += dot(gated, sc, TN)
        acc_b[...] += jnp.sum(dz.astype(F32), axis=0, keepdims=True)
        resid[s, :] = (hist[s, :].astype(F32) + dot(gated, res_w[...])).astype(BF16)
        skipped[s, :] = dot(gated, skip_w[...]).astype(BF16)
        gi_part[s, :] = oc.astype(F32) + dot(dz, now_w[...], NT)
        return carry

    lax.fori_loop(0, K, step, 0)

    r1 = BIAS_ROWS
    r2 = r1 + hg
    r3 = r2 + Rn
    r4 = r3 + Rn
    for q in range(D):
        blk = b_own.at[q // 2, q % 2]
        blk[0:BIAS_ROWS, :] = jnp.zeros((BIAS_ROWS, W), F32)
        blk[0:1, 0:bw] = acc_b[:, q * bw:(q + 1) * bw]
        blk[r1:r2, 0:2 * C] = acc_rs[q * Rg:q * Rg + hg, :]
        blk[r1:r2, 2 * C:] = acc_rs[q * Rg + hg:(q + 1) * Rg, :]
        blk[r2:r3, :] = acc_np[q * Rn:(q + 1) * Rn, :]
        blk[r3:r4, :] = acc_np[C + q * Rn:C + (q + 1) * Rn, :]

    for j in range(H):
        a_send[j] = b_own[j, 1 - par].astype(BF16)
    core = remote(a_send, a_recv, a_ss, a_rs, {"dp": 2 * j0 + 1 - par})
    core.start()
    core.wait_recv()

    zs = []
    for o in range(1, H):
        jt = lax.rem(j0 + o, H)
        b_send[o - 1] = (b_own[jt, par] + a_recv[jt].astype(F32)).astype(BF16)
        cp = remote(b_send.at[o - 1], b_recv.at[o - 1], b_ss.at[o - 1], b_rs.at[o - 1], {"dp": 2 * jt + par})
        cp.start()
        zs.append(cp)
    total = b_own[j0, par] + a_recv[j0].astype(F32)
    for o in range(1, H):
        zs[o - 1].wait_recv()
        total = total + b_recv[o - 1].astype(F32)
    for t in range(T):
        tot[t] = total[:, t * lane:(t + 1) * lane]

    cs = []
    for o in range(1, T):
        t = lax.rem(me + o, T)
        c_send[o - 1] = tot[t].astype(BF16)
        cp = remote(c_send.at[o - 1], c_recv.at[o - 1], c_ss.at[o - 1], c_rs.at[o - 1], {"tm": t})
        cp.start()
        cs.append(cp)
    mine = tot[me]
    for o in range(1, T):
        cs[o - 1].wait_recv()
        mine = mine + c_recv[o - 1].astype(F32)
    d_buf[me] = mine.astype(BF16)
    ds = []
    for o in range(1, T):
        cp = remote(d_buf.at[me], d_buf.at[me], d_ss.at[o - 1], d_rs.at[o - 1], {"tm": lax.rem(me + o, T)})
        cp.start()
        ds.append(cp)

    def finish(c, carry):
        s = pl.ds(pl.multiple_of(c * CHUNK, CHUNK), CHUNK)

        @pl.when(has_next)
        def _():
            bwd(c).wait_recv()
            fwd(c).wait_send()

        grad_in[s, :] = (gi_part[s, :] + bw_recv[s, :].astype(F32)).astype(BF16)

        @pl.when(has_prev)
        def _():
            bwd(c).wait_send()

        return carry

    lax.fori_loop(0, K, finish, 0)

    for o in range(1, T):
        t = lax.rem(me + T - o, T)
        remote(d_buf.at[t], d_buf.at[t], d_ss.at[o - 1], d_rs.at[o - 1], {"tm": lax.rem(me + o, T)}).wait_recv()
    full = jnp.concatenate([d_buf[t] for t in range(T)], axis=1).astype(F32)
    g_bias[...] = full[0:1, 0:bw]
    for half in range(2):
        at = 2 * C * half
        g_res[half * hg:(half + 1) * hg, :] = full[r1:r2, at:at + C]
        g_skip[half * hg:(half + 1) * hg, :] = full[r1:r2, at + C:at + 2 * C]
    g_now[...] = full[r2:r3, :]
    g_past[...] = full[r3:r4, :]

    core.wait_send()
    for cp in zs + cs + ds:
        cp.wait_send()


def shards(T, D, history, now_weight, past_weight, gate_bias, residual_weight, skip_weight,
           out_cotangent, skip_cotangent):
    histories, steps, C = history.shape
    assert steps == DILATION_STEPS
    rows = histories * steps
    G = residual_weight.shape[0]
    W = 2 * G
    K = rows // CHUNK
    H = D // 2
    R = BIAS_ROWS + G // D // 2 + 2 * (C // D)
    lane = W // T
    flat = [x.reshape(rows, C) for x in (history, out_cotangent, skip_cotangent)]
    vmem = pl.BlockSpec(memory_space=pltpu.VMEM)
    dma = pltpu.SemaphoreType.DMA
    V = pltpu.VMEM
    outs = pl.pallas_call(
        functools.partial(layer_kernel, T, D),
        out_shape=[
            jax.ShapeDtypeStruct((rows, C), BF16),
            jax.ShapeDtypeStruct((rows, C), BF16),
            jax.ShapeDtypeStruct((rows, C), BF16),
            jax.ShapeDtypeStruct((C // D, W), F32),
            jax.ShapeDtypeStruct((C // D, W), F32),
            jax.ShapeDtypeStruct((1, W // D), F32),
            jax.ShapeDtypeStruct((G // D, C), F32),
            jax.ShapeDtypeStruct((G // D, C), F32),
        ],
        in_specs=[vmem] * 8,
        out_specs=[vmem] * 8,
        scratch_shapes=[
            V((rows, C), BF16), V((rows, C), BF16), V((rows, C), BF16), V((rows, C), F32),
            V((CHUNK, W), F32), V((CHUNK, G), F32),
            V((2 * C, W), F32), V((G, 2 * C), F32), V((1, W), F32),
            V((H, R, W), BF16), V((H, R, W), BF16), V((H, 2, R, W), F32),
            V((H - 1, R, W), BF16), V((H - 1, R, W), BF16),
            V((T, R, lane), F32), V((T - 1, R, lane), BF16), V((T - 1, R, lane), BF16),
            V((T, R, lane), BF16),
            dma((K,)), dma((K,)), dma((K,)), dma((K,)), dma, dma,
            dma((H - 1,)), dma((H - 1,)), dma((T - 1,)), dma((T - 1,)), dma((T - 1,)), dma((T - 1,)),
        ],
        compiler_params=pltpu.CompilerParams(
            collective_id=0, has_side_effects=True, vmem_limit_bytes=60 * 1024 * 1024
        ),
        cost_estimate=pl.CostEstimate(
            flops=rows * C * G * 36, bytes_accessed=rows * C * 12, transcendentals=rows * W
        ),
        name="gated_layer",
    )(flat[0], now_weight, past_weight, gate_bias.reshape(1, W), residual_weight, skip_weight, flat[1], flat[2])
    shape = (histories, steps, C)
    return (
        outs[0].reshape(shape), outs[1].reshape(shape), outs[2].reshape(shape),
        outs[3], outs[4], outs[5].reshape(W // D), outs[6], outs[7],
    )


def solution(mesh):
    seq = P("dp", "tm", None)
    return jax.shard_map(
        functools.partial(shards, mesh.shape["tm"], mesh.shape["dp"]),
        mesh=mesh,
        in_specs=(seq, P(), P(), P(), P(), P(), seq, seq),
        out_specs=(seq, seq, seq, P("dp", None), P("dp", None), P("dp"), P("dp", None), P("dp", None)),
        check_vma=False,
    )
```

```python
import functools

import jax
import jax.numpy as jnp
from jax import lax
from jax.experimental import pallas as pl
from jax.experimental.pallas import tpu as pltpu
from jax.sharding import PartitionSpec as P

DILATION_STEPS = 2048
CHUNK = 512
BIAS_ROWS = 16
F32 = jnp.float32
BF16 = jnp.bfloat16
MESH = pl.DeviceIdType.MESH


def dot(a, b, dims=((1,), (0,))):
    return lax.dot_general(a, b, (dims, ((), ())), preferred_element_type=F32)


NT = ((1,), (1,))
TN = ((0,), (0,))


def layer_kernel(
    T, D,
    hist, now_w, past_w, bias, res_w, skip_w, ocot, scot,
    resid, skipped, grad_in, packed,
    delayed, bw_send, bw_recv, relay_f, relay_b, gi_part, zn, dgs, gated_s, dz_s,
    acc_np, acc_rs, acc_b, a_send, a_recv, b_own, b_send, b_recv, tot, c_send, c_recv, d_buf,
    f_ss, f_rs, w_ss, w_rs, rf_ss, rf_rs, rb_ss, rb_rs,
    a_ss, a_rs, b_ss, b_rs, c_ss, c_rs, d_ss, d_rs,
):
    rows, C = hist.shape
    G = res_w.shape[0]
    H = D // 2
    K = rows // CHUNK
    me = lax.axis_index("tm")
    dp = lax.axis_index("dp")
    par = lax.rem(dp, 2)
    j0 = dp // 2
    up = lax.rem(me + 1, T)
    down = lax.rem(me + T - 1, T)
    up2 = lax.rem(me + 2, T)
    down2 = lax.rem(me + T - 2, T)
    has_prev = me > 0
    has_next = me < T - 1
    odd = lax.rem(me, 2) == 1
    even = lax.rem(me, 2) == 0
    Rn = C // D
    Rg = G // D
    hg = Rg // 2
    W = 2 * G
    bw = W // D
    lane = W // T
    r1, r2, r3, r4 = marks(C, G, D)
    pieces = [(0, r1), (r1, r3), (r3, r4)]

    barrier = pltpu.get_barrier_semaphore()
    for o in range(1, T):
        pl.semaphore_signal(barrier, inc=1, device_id={"tm": lax.rem(me + o, T)}, device_id_type=MESH)
    for o in range(1, H):
        pl.semaphore_signal(
            barrier, inc=1, device_id={"dp": 2 * lax.rem(j0 + o, H) + par}, device_id_type=MESH
        )
    pl.semaphore_signal(barrier, inc=1, device_id={"dp": 2 * j0 + 1 - par}, device_id_type=MESH)
    pl.semaphore_wait(barrier, T - 1 + H)

    def remote(src, dst, ss, rs, target):
        return pltpu.make_async_remote_copy(
            src_ref=src, dst_ref=dst, send_sem=ss, recv_sem=rs, device_id=target, device_id_type=MESH
        )

    def span(c):
        if isinstance(c, int):
            return pl.ds(c * CHUNK, CHUNK)
        return pl.ds(pl.multiple_of(c * CHUNK, CHUNK), CHUNK)

    def fwd(c):
        return remote(hist.at[span(c)], delayed.at[span(c)], f_ss.at[c], f_rs.at[c], {"tm": up})

    def fwd_in(r):
        return remote(hist.at[span(2 * r + 1)], relay_f.at[r], f_ss.at[2 * r + 1], rf_rs.at[r], {"tm": up2})

    def fwd_out(r):
        return remote(relay_f.at[r], delayed.at[span(2 * r + 1)], rf_ss.at[r], f_rs.at[2 * r + 1], {"tm": down})

    def bwd(c):
        return remote(bw_send.at[span(c)], bw_recv.at[span(c)], w_ss.at[c], w_rs.at[c], {"tm": down})

    def bwd_in(r):
        return remote(bw_send.at[span(2 * r + 1)], relay_b.at[r], w_ss.at[2 * r + 1], rb_rs.at[r], {"tm": down2})

    def bwd_out(r):
        return remote(relay_b.at[r], bw_recv.at[span(2 * r + 1)], rb_ss.at[r], w_rs.at[2 * r + 1], {"tm": up})

    relays_f = jnp.logical_and(odd, me >= 3)
    relays_b = jnp.logical_and(even, me < T - 2)
    for c in range(K):
        if c % 2 == 0:
            @pl.when(has_next)
            def _():
                fwd(c).start()
        else:
            @pl.when(even)
            def _():
                fwd(c).start()

            @pl.when(jnp.logical_and(odd, has_next))
            def _():
                fwd_in(c // 2).start()

    @pl.when(me == 0)
    def _():
        delayed[...] = jnp.zeros_like(delayed)

    @pl.when(me == T - 1)
    def _():
        bw_recv[...] = jnp.zeros_like(bw_recv)

    acc_np[...] = jnp.zeros_like(acc_np)
    acc_rs[...] = jnp.zeros_like(acc_rs)
    acc_b[...] = jnp.zeros_like(acc_b)

    def before(c):
        s = span(c)
        zn[...] = dot(hist[s, :], now_w[...]) + bias[...]
        dgs[...] = dot(ocot[s, :], res_w[...], NT) + dot(scot[s, :], skip_w[...], NT)

    def late(c):
        s = span(c)
        gated = gated_s[...]
        resid[s, :] = (hist[s, :].astype(F32) + dot(gated, res_w[...])).astype(BF16)
        skipped[s, :] = dot(gated, skip_w[...]).astype(BF16)
        gi_part[s, :] = ocot[s, :].astype(F32) + dot(dz_s[...], now_w[...], NT)

    def core_part(c):
        s = span(c)

        @pl.when(has_prev)
        def _():
            fwd(c).wait_recv()

        z = zn[...] + dot(delayed[s, :], past_w[...])
        th = jnp.tanh(z[:, :G])
        sg = 0.5 * jnp.tanh(0.5 * z[:, G:]) + 0.5
        ts = th * sg
        gated_s[...] = ts.astype(BF16)
        dg = dgs[...]
        dz_s[:, :G] = (dg * sg * (1.0 - th * th)).astype(BF16)
        dz_s[:, G:] = (dg * ts * (1.0 - sg)).astype(BF16)
        bw_send[s, :] = dot(dz_s[...], past_w[...], NT).astype(BF16)

    def add_rs(c):
        s = span(c)
        acc_rs[:, 0:C] += dot(gated_s[...], ocot[s, :], TN)
        acc_rs[:, C:] += dot(gated_s[...], scot[s, :], TN)

    def add_now(c):
        acc_np[0:C, :] += dot(hist[span(c), :], dz_s[...], TN)
        acc_b[...] += jnp.sum(dz_s[...].astype(F32), axis=0, keepdims=True)

    def add_past(c):
        acc_np[C:, :] += dot(delayed[span(c), :], dz_s[...], TN)

    def pair(g, carry):
        for half in range(2):
            c = 2 * g + half
            before(c)
            if half == 1:
                late(c - 1)
            else:
                @pl.when(c > 0)
                def _():
                    late(c - 1)

            @pl.when(jnp.logical_and(relays_f, jnp.logical_and(c > 0, c <= K // 2)))
            def _():
                fwd_in(c - 1).wait_recv()
                fwd_out(c - 1).start()

            core_part(c)
            if half == 0:
                @pl.when(odd)
                def _():
                    bwd(c).start()
            else:
                @pl.when(odd)
                def _():
                    bwd(c).start()

                @pl.when(jnp.logical_and(even, has_prev))
                def _():
                    bwd_in(g).start()

            @pl.when(c < K - 1)
            def _():
                add_rs(c)
                add_now(c)
                add_past(c)

        return carry

    lax.fori_loop(0, K // 2, pair, 0)

    @pl.when(jnp.logical_and(even, has_prev))
    def _():
        for r in range(K // 2):
            bwd(2 * r).start()

    cores = []

    def core_send(p):
        lo, hi = pieces[p]
        for j in range(H):
            a_send[j, lo:hi, :] = b_own[j, 1 - par, lo:hi, :].astype(BF16)
        cp = remote(a_send.at[:, lo:hi, :], a_recv.at[:, lo:hi, :], a_ss.at[p], a_rs.at[p],
                    {"dp": 2 * j0 + 1 - par})
        cp.start()
        cores.append(cp)

    zs = []

    def z_send(p):
        lo, hi = pieces[p]
        cores[p].wait_recv()
        for o in range(1, H):
            jt = lax.rem(j0 + o, H)
            b_send[o - 1, lo:hi, :] = (
                b_own[jt, par, lo:hi, :] + a_recv[jt, lo:hi, :].astype(F32)
            ).astype(BF16)
            cp = remote(b_send.at[o - 1, lo:hi, :], b_recv.at[o - 1, lo:hi, :],
                        b_ss.at[p, o - 1], b_rs.at[p, o - 1], {"dp": 2 * jt + par})
            cp.start()
            zs.append(cp)

    last = K - 1
    add_rs(last)
    for q in range(D):
        b_own[q // 2, q % 2, 0:r1, 0:2 * C] = acc_rs[q * Rg:q * Rg + hg, :]
        b_own[q // 2, q % 2, 0:r1, 2 * C:] = acc_rs[q * Rg + hg:(q + 1) * Rg, :]
    core_send(0)
    add_now(last)
    for q in range(D):
        blk = b_own.at[q // 2, q % 2]
        blk[r1:r2, :] = jnp.zeros((BIAS_ROWS, W), F32)
        blk[r1:r1 + 1, 0:bw] = acc_b[:, q * bw:(q + 1) * bw]
        blk[r2:r3, :] = acc_np[q * Rn:(q + 1) * Rn, :]
    core_send(1)
    z_send(0)
    add_past(last)
    for q in range(D):
        b_own[q // 2, q % 2, r3:r4, :] = acc_np[C + q * Rn:C + (q + 1) * Rn, :]
    core_send(2)
    z_send(1)
    z_send(2)
    late(last)

    @pl.when(relays_b)
    def _():
        for r in range(K // 2):
            bwd_in(r).wait_recv()
            bwd_out(r).start()

    cs = []
    for p, (lo, hi) in enumerate(pieces):
        total = b_own[j0, par, lo:hi, :] + a_recv[j0, lo:hi, :].astype(F32)
        for o in range(1, H):
            zs[p * (H - 1) + o - 1].wait_recv()
            total = total + b_recv[o - 1, lo:hi, :].astype(F32)
        for t in range(T):
            tot[t, lo:hi, :] = total[:, t * lane:(t + 1) * lane]
        for o in range(1, T):
            t = lax.rem(me + o, T)
            c_send[o - 1, lo:hi, :] = tot[t, lo:hi, :].astype(BF16)
            cp = remote(c_send.at[o - 1, lo:hi, :], c_recv.at[o - 1, lo:hi, :],
                        c_ss.at[p, o - 1], c_rs.at[p, o - 1], {"tm": t})
            cp.start()
            cs.append(cp)

    ds = []
    for p, (lo, hi) in enumerate(pieces):
        mine = tot[me, lo:hi, :]
        for o in range(1, T):
            cs[p * (T - 1) + o - 1].wait_recv()
            mine = mine + c_recv[o - 1, lo:hi, :].astype(F32)
        d_buf[me, lo:hi, :] = mine.astype(BF16)
        for o in range(1, T):
            cp = remote(d_buf.at[me, lo:hi, :], d_buf.at[me, lo:hi, :], d_ss.at[p, o - 1], d_rs.at[p, o - 1],
                        {"tm": lax.rem(me + o, T)})
            cp.start()
            ds.append(cp)

    def finish(c, carry):
        s = span(c)

        @pl.when(has_next)
        def _():
            bwd(c).wait_recv()
            fwd(c).wait_send()

        grad_in[s, :] = (gi_part[s, :] + bw_recv[s, :].astype(F32)).astype(BF16)

        @pl.when(has_prev)
        def _():
            bwd(c).wait_send()

        return carry

    lax.fori_loop(0, K, finish, 0)

    for p, (lo, hi) in enumerate(pieces):
        for o in range(1, T):
            t = lax.rem(me + T - o, T)
            remote(d_buf.at[t, lo:hi, :], d_buf.at[t, lo:hi, :], d_ss.at[p, o - 1], d_rs.at[p, o - 1],
                   {"tm": lax.rem(me + o, T)}).wait_recv()
    for t in range(T):
        packed[:, t * lane:(t + 1) * lane] = d_buf[t]

    @pl.when(relays_f)
    def _():
        for r in range(K // 2):
            fwd_out(r).wait_send()

    @pl.when(relays_b)
    def _():
        for r in range(K // 2):
            bwd_out(r).wait_send()

    for cp in cores + zs + cs + ds:
        cp.wait_send()


def marks(C, G, D):
    r1 = G // D // 2
    r2 = r1 + BIAS_ROWS
    r3 = r2 + C // D
    return r1, r2, r3, r3 + C // D


def unpack_kernel(D, a, b, c, packed, oa, ob, oc, g_now, g_past, g_bias, g_res, g_skip, sems):
    copies = [pltpu.make_async_copy(x, y, sems.at[i]) for i, (x, y) in enumerate(((a, oa), (b, ob), (c, oc)))]
    for cp in copies:
        cp.start()
    C = a.shape[1]
    G = packed.shape[1] // 2
    r1, r2, r3, r4 = marks(C, G, D)
    g_bias[...] = packed[r1:r2, 0:2 * G // D].astype(F32)[0:1]
    for half in range(2):
        at = 2 * C * half
        g_res[half * r1:(half + 1) * r1, :] = packed[0:r1, at:at + C].astype(F32)
        g_skip[half * r1:(half + 1) * r1, :] = packed[0:r1, at + C:at + 2 * C].astype(F32)
    g_now[...] = packed[r2:r3, :].astype(F32)
    g_past[...] = packed[r3:r4, :].astype(F32)
    for cp in copies:
        cp.wait()


def shards(T, D, history, now_weight, past_weight, gate_bias, residual_weight, skip_weight,
           out_cotangent, skip_cotangent):
    histories, steps, C = history.shape
    assert steps == DILATION_STEPS
    rows = histories * steps
    G = residual_weight.shape[0]
    W = 2 * G
    K = rows // CHUNK
    H = D // 2
    R = marks(C, G, D)[3]
    lane = W // T
    flat = [x.reshape(rows, C) for x in (history, out_cotangent, skip_cotangent)]
    vmem = pl.BlockSpec(memory_space=pltpu.VMEM)
    hbm = pl.BlockSpec(memory_space=pl.ANY)
    dma = pltpu.SemaphoreType.DMA
    V = pltpu.VMEM
    seq = jax.ShapeDtypeStruct((rows, C), BF16)
    parts = pl.pallas_call(
        functools.partial(layer_kernel, T, D),
        out_shape=[seq, seq, seq, jax.ShapeDtypeStruct((R, W), BF16)],
        in_specs=[vmem] * 8,
        out_specs=[vmem] * 4,
        scratch_shapes=[
            V((rows, C), BF16), V((rows, C), BF16), V((rows, C), BF16),
            V((K // 2, CHUNK, C), BF16), V((K // 2, CHUNK, C), BF16), V((rows, C), F32),
            V((CHUNK, W), F32), V((CHUNK, G), F32), V((CHUNK, G), BF16), V((CHUNK, W), BF16),
            V((2 * C, W), F32), V((G, 2 * C), F32), V((1, W), F32),
            V((H, R, W), BF16), V((H, R, W), BF16), V((H, 2, R, W), F32),
            V((H - 1, R, W), BF16), V((H - 1, R, W), BF16),
            V((T, R, lane), F32), V((T - 1, R, lane), BF16), V((T - 1, R, lane), BF16),
            V((T, R, lane), BF16),
            dma((K,)), dma((K,)), dma((K,)), dma((K,)),
            dma((K // 2,)), dma((K // 2,)), dma((K // 2,)), dma((K // 2,)),
            dma((3,)), dma((3,)), dma((3, H - 1)), dma((3, H - 1)),
            dma((3, T - 1)), dma((3, T - 1)), dma((3, T - 1)), dma((3, T - 1)),
        ],
        compiler_params=pltpu.CompilerParams(
            collective_id=0, has_side_effects=True, vmem_limit_bytes=(28 + rows // 256) * 1024 * 1024
        ),
        cost_estimate=pl.CostEstimate(
            flops=rows * C * G * 36, bytes_accessed=rows * C * 12, transcendentals=rows * W
        ),
        name="gated_layer",
    )(flat[0], now_weight, past_weight, gate_bias.reshape(1, W), residual_weight, skip_weight, flat[1], flat[2])
    outs = pl.pallas_call(
        functools.partial(unpack_kernel, D),
        out_shape=[
            seq, seq, seq,
            jax.ShapeDtypeStruct((C // D, W), F32),
            jax.ShapeDtypeStruct((C // D, W), F32),
            jax.ShapeDtypeStruct((1, W // D), F32),
            jax.ShapeDtypeStruct((G // D, C), F32),
            jax.ShapeDtypeStruct((G // D, C), F32),
        ],
        in_specs=[hbm] * 3 + [vmem],
        out_specs=[hbm] * 3 + [vmem] * 5,
        scratch_shapes=[dma((3,))],
        compiler_params=pltpu.CompilerParams(vmem_limit_bytes=8 * 1024 * 1024),
        cost_estimate=pl.CostEstimate(flops=0, bytes_accessed=rows * C * 12, transcendentals=0),
        name="unpack_results",
    )(*parts)
    shape = (histories, steps, C)
    return (
        outs[0].reshape(shape), outs[1].reshape(shape), outs[2].reshape(shape),
        outs[3], outs[4], outs[5].reshape(W // D), outs[6], outs[7],
    )


def solution(mesh):
    seq = P("dp", "tm", None)
    return jax.shard_map(
        functools.partial(shards, mesh.shape["tm"], mesh.shape["dp"]),
        mesh=mesh,
        in_specs=(seq, P(), P(), P(), P(), P(), seq, seq),
        out_specs=(seq, seq, seq, P("dp", None), P("dp", None), P("dp"), P("dp", None), P("dp", None)),
        check_vma=False,
    )
```

```python
import functools

import jax
import jax.numpy as jnp
from jax import lax
from jax.experimental import pallas as pl
from jax.experimental.pallas import tpu as pltpu
from jax.sharding import PartitionSpec as P

DILATION_STEPS = 2048
CHUNK = 512
BIAS_ROWS = 16
F32 = jnp.float32
BF16 = jnp.bfloat16
MESH = pl.DeviceIdType.MESH


def dot(a, b, dims=((1,), (0,))):
    return lax.dot_general(a, b, (dims, ((), ())), preferred_element_type=F32)


NT = ((1,), (1,))
TN = ((0,), (0,))


def layer_kernel(
    T, D,
    hist_h, now_h, past_h, bias_h, res_h, skip_h, ocot_h, scot_h,
    resid_h, skipped_h, grad_in_h, packed,
    hist, now_w, past_w, bias, res_w, skip_w, ocot, scot, resid, skipped, grad_in,
    delayed, bw_send, bw_recv, gi_part, zn, dgs, gated_s, dz_s,
    acc_np, acc_rs, acc_b, a_send, a_recv, b_own, y_send, y_recv, b_send, b_recv,
    tot, c_send, c_recv, d_buf,
    in_s, out_s, f_ss, f_rs, w_ss, w_rs,
    a_ss, a_rs, y_ss, y_rs, b_ss, b_rs, c_ss, c_rs, d_ss, d_rs,
):
    rows, C = hist.shape
    G = res_w.shape[0]
    H = D // 2
    K = rows // CHUNK
    S = T // 2
    me = lax.axis_index("tm")
    dp = lax.axis_index("dp")
    par = lax.rem(dp, 2)
    j0 = dp // 2
    up = lax.rem(me + 1, T)
    down = lax.rem(me + T - 1, T)
    has_prev = me > 0
    has_next = me < T - 1
    yb = lax.rem(me // 2, 2)
    across = me + 2 - 4 * yb
    gi = 2 * (me // 4) + lax.rem(me, 2)
    Rn = C // D
    Rg = G // D
    hg = Rg // 2
    W = 2 * G
    bw = W // D
    lane = W // T
    r1, r2, r3, r4 = marks(C, G, D)
    pieces = [(0, r1), (r1, r3), (r3, r4)]

    loads = [
        pltpu.make_async_copy(x, y, in_s.at[i])
        for i, (x, y) in enumerate((
            (hist_h, hist), (now_h, now_w), (ocot_h, ocot), (scot_h, scot),
            (res_h, res_w), (skip_h, skip_w), (past_h, past_w), (bias_h, bias),
        ))
    ]
    for cp in loads:
        cp.start()

    barrier = pltpu.get_barrier_semaphore()
    for o in range(1, T):
        pl.semaphore_signal(barrier, inc=1, device_id={"tm": lax.rem(me + o, T)}, device_id_type=MESH)
    for o in range(1, H):
        pl.semaphore_signal(
            barrier, inc=1, device_id={"dp": 2 * lax.rem(j0 + o, H) + par}, device_id_type=MESH
        )
    pl.semaphore_signal(barrier, inc=1, device_id={"dp": 2 * j0 + 1 - par}, device_id_type=MESH)

    @pl.when(me == 0)
    def _():
        delayed[...] = jnp.zeros_like(delayed)

    @pl.when(me == T - 1)
    def _():
        bw_recv[...] = jnp.zeros_like(bw_recv)

    acc_np[...] = jnp.zeros_like(acc_np)
    acc_rs[...] = jnp.zeros_like(acc_rs)
    acc_b[...] = jnp.zeros_like(acc_b)
    pl.semaphore_wait(barrier, T - 1 + H)

    def remote(src, dst, ss, rs, target):
        return pltpu.make_async_remote_copy(
            src_ref=src, dst_ref=dst, send_sem=ss, recv_sem=rs, device_id=target, device_id_type=MESH
        )

    def span(c):
        if isinstance(c, int):
            return pl.ds(c * CHUNK, CHUNK)
        return pl.ds(pl.multiple_of(c * CHUNK, CHUNK), CHUNK)

    def fwd(c):
        return remote(hist_h.at[span(c)], delayed.at[span(c)], f_ss.at[c], f_rs.at[c], {"tm": up})

    def bwd(c):
        return remote(bw_send.at[span(c)], bw_recv.at[span(c)], w_ss.at[c], w_rs.at[c], {"tm": down})

    def store(i, c):
        src, dst = ((resid, resid_h), (skipped, skipped_h), (grad_in, grad_in_h))[i]
        return pltpu.make_async_copy(src.at[span(c)], dst.at[span(c)], out_s.at[i, c])

    @pl.when(has_next)
    def _():
        for c in range(K):
            fwd(c).start()

    for cp in loads:
        cp.wait()

    def before(c):
        s = span(c)
        zn[...] = dot(hist[s, :], now_w[...]) + bias[...]
        dgs[...] = dot(ocot[s, :], res_w[...], NT) + dot(scot[s, :], skip_w[...], NT)

    def late(c):
        s = span(c)
        gated = gated_s[...]
        resid[s, :] = (hist[s, :].astype(F32) + dot(gated, res_w[...])).astype(BF16)
        skipped[s, :] = dot(gated, skip_w[...]).astype(BF16)
        gi_part[s, :] = ocot[s, :].astype(F32) + dot(dz_s[...], now_w[...], NT)
        store(0, c).start()
        store(1, c).start()

    def core_part(c):
        s = span(c)

        @pl.when(has_prev)
        def _():
            fwd(c).wait_recv()

        z = zn[...] + dot(delayed[s, :], past_w[...])
        th = jnp.tanh(z[:, :G])
        sg = 0.5 * jnp.tanh(0.5 * z[:, G:]) + 0.5
        ts = th * sg
        gated_s[...] = ts.astype(BF16)
        dg = dgs[...]
        dz_s[:, :G] = (dg * sg * (1.0 - th * th)).astype(BF16)
        dz_s[:, G:] = (dg * ts * (1.0 - sg)).astype(BF16)
        bw_send[s, :] = dot(dz_s[...], past_w[...], NT).astype(BF16)

    def add_rs(c):
        s = span(c)
        acc_rs[:, 0:C] += dot(gated_s[...], ocot[s, :], TN)
        acc_rs[:, C:] += dot(gated_s[...], scot[s, :], TN)

    def add_now(c):
        acc_np[0:C, :] += dot(hist[span(c), :], dz_s[...], TN)
        acc_b[...] += jnp.sum(dz_s[...].astype(F32), axis=0, keepdims=True)

    def add_past(c):
        acc_np[C:, :] += dot(delayed[span(c), :], dz_s[...], TN)

    def step(c, carry):
        before(c)
        core_part(c)
        add_rs(c)
        add_now(c)
        add_past(c)
        late(c)
        return carry

    last = K - 1
    lax.fori_loop(0, last, step, 0)
    before(last)
    core_part(last)

    @pl.when(has_prev)
    def _():
        for c in range(K):
            bwd(c).start()

    cores, ys, zs, cs, ds = [], [], [], [], []

    def core_send(p):
        lo, hi = pieces[p]
        for j in range(H):
            for h in range(2):
                a_send[j, h, lo:hi, :] = b_own[j, 1 - par, h, lo:hi, :].astype(BF16)
        cp = remote(a_send.at[:, :, lo:hi, :], a_recv.at[:, :, lo:hi, :], a_ss.at[p], a_rs.at[p],
                    {"dp": 2 * j0 + 1 - par})
        cp.start()
        cores.append(cp)

    def y_stage(p):
        lo, hi = pieces[p]
        cores[p].wait_recv()
        for j in range(H):
            y_send[j, lo:hi, :] = (
                b_own[j, par, 1 - yb, lo:hi, :] + a_recv[j, 1 - yb, lo:hi, :].astype(F32)
            ).astype(BF16)
        cp = remote(y_send.at[:, lo:hi, :], y_recv.at[:, lo:hi, :], y_ss.at[p], y_rs.at[p], {"tm": across})
        cp.start()
        ys.append(cp)

    def pair_sum(j, lo, hi):
        own = b_own[j, par, yb, lo:hi, :] + a_recv[j, yb, lo:hi, :].astype(F32)
        return own + y_recv[j, lo:hi, :].astype(F32)

    def z_send(p):
        lo, hi = pieces[p]
        ys[p].wait_recv()
        for o in range(1, H):
            jt = lax.rem(j0 + o, H)
            b_send[o - 1, lo:hi, :] = pair_sum(jt, lo, hi).astype(BF16)
            cp = remote(b_send.at[o - 1, lo:hi, :], b_recv.at[o - 1, lo:hi, :],
                        b_ss.at[p, o - 1], b_rs.at[p, o - 1], {"dp": 2 * jt + par})
            cp.start()
            zs.append(cp)

    def put(q, lo, hi, lanes, value):
        h = lanes // G
        at = lanes - h * G
        b_own[q // 2, q % 2, h, lo:hi, at:at + value.shape[1]] = value

    add_rs(last)
    for q in range(D):
        put(q, 0, r1, 0, acc_rs[q * Rg:q * Rg + hg, :])
        put(q, 0, r1, G, acc_rs[q * Rg + hg:(q + 1) * Rg, :])
    core_send(0)
    add_now(last)
    for q in range(D):
        for h in range(2):
            put(q, r1, r2, h * G, jnp.zeros((BIAS_ROWS, G), F32))
            put(q, r2, r3, h * G, acc_np[q * Rn:(q + 1) * Rn, h * G:(h + 1) * G])
        put(q, r1, r1 + 1, 0, acc_b[:, q * bw:(q + 1) * bw])
    core_send(1)
    y_stage(0)
    add_past(last)
    for q in range(D):
        for h in range(2):
            put(q, r3, r4, h * G, acc_np[C + q * Rn:C + (q + 1) * Rn, h * G:(h + 1) * G])
    core_send(2)
    y_stage(1)
    z_send(0)
    y_stage(2)
    z_send(1)
    late(last)
    z_send(2)

    for p, (lo, hi) in enumerate(pieces):
        total = pair_sum(j0, lo, hi)
        for o in range(1, H):
            zs[p * (H - 1) + o - 1].wait_recv()
            total = total + b_recv[o - 1, lo:hi, :].astype(F32)
        for g in range(S):
            tot[g, lo:hi, :] = total[:, g * lane:(g + 1) * lane]
        for o in range(1, S):
            g = lax.rem(gi + o, S)
            c_send[o - 1, lo:hi, :] = tot[g, lo:hi, :].astype(BF16)
            cp = remote(c_send.at[o - 1, lo:hi, :], c_recv.at[o - 1, lo:hi, :],
                        c_ss.at[p, o - 1], c_rs.at[p, o - 1],
                        {"tm": 4 * (g // 2) + 2 * yb + lax.rem(g, 2)})
            cp.start()
            cs.append(cp)

    slot = yb * S + gi
    for p, (lo, hi) in enumerate(pieces):
        mine = tot[gi, lo:hi, :]
        for o in range(1, S):
            cs[p * (S - 1) + o - 1].wait_recv()
            mine = mine + c_recv[o - 1, lo:hi, :].astype(F32)
        d_buf[slot, lo:hi, :] = mine.astype(BF16)
        for o in range(1, T):
            cp = remote(d_buf.at[slot, lo:hi, :], d_buf.at[slot, lo:hi, :], d_ss.at[p, o - 1], d_rs.at[p, o - 1],
                        {"tm": lax.rem(me + o, T)})
            cp.start()
            ds.append(cp)

    def finish(c, carry):
        s = span(c)

        @pl.when(has_next)
        def _():
            bwd(c).wait_recv()
            fwd(c).wait_send()

        grad_in[s, :] = (gi_part[s, :] + bw_recv[s, :].astype(F32)).astype(BF16)
        store(2, c).start()
        store(0, c).wait()
        store(1, c).wait()

        @pl.when(has_prev)
        def _():
            bwd(c).wait_send()

        return carry

    lax.fori_loop(0, K, finish, 0)

    for p, (lo, hi) in enumerate(pieces):
        for o in range(1, T):
            t = lax.rem(me + T - o, T)
            at = lax.rem(t // 2, 2) * S + 2 * (t // 4) + lax.rem(t, 2)
            remote(d_buf.at[at, lo:hi, :], d_buf.at[at, lo:hi, :], d_ss.at[p, o - 1], d_rs.at[p, o - 1],
                   {"tm": lax.rem(me + o, T)}).wait_recv()
    for t in range(T):
        packed[:, t * lane:(t + 1) * lane] = d_buf[t]
    for cp in cores + ys + zs + cs + ds:
        cp.wait_send()
    for c in range(K):
        store(2, c).wait()


def marks(C, G, D):
    r1 = G // D // 2
    r2 = r1 + BIAS_ROWS
    r3 = r2 + C // D
    return r1, r2, r3, r3 + C // D


def unpack_kernel(D, a, b, c, packed, oa, ob, oc, g_now, g_past, g_bias, g_res, g_skip, sems):
    copies = [pltpu.make_async_copy(x, y, sems.at[i]) for i, (x, y) in enumerate(((a, oa), (b, ob), (c, oc)))]
    for cp in copies:
        cp.start()
    C = a.shape[1]
    G = packed.shape[1] // 2
    r1, r2, r3, r4 = marks(C, G, D)
    g_bias[...] = packed[r1:r2, 0:2 * G // D].astype(F32)[0:1]
    for half in range(2):
        at = 2 * C * half
        g_res[half * r1:(half + 1) * r1, :] = packed[0:r1, at:at + C].astype(F32)
        g_skip[half * r1:(half + 1) * r1, :] = packed[0:r1, at + C:at + 2 * C].astype(F32)
    g_now[...] = packed[r2:r3, :].astype(F32)
    g_past[...] = packed[r3:r4, :].astype(F32)
    for cp in copies:
        cp.wait()


def shards(T, D, history, now_weight, past_weight, gate_bias, residual_weight, skip_weight,
           out_cotangent, skip_cotangent):
    histories, steps, C = history.shape
    assert steps == DILATION_STEPS
    rows = histories * steps
    G = residual_weight.shape[0]
    W = 2 * G
    K = rows // CHUNK
    H = D // 2
    R = marks(C, G, D)[3]
    lane = W // T
    S = T // 2
    flat = [x.reshape(rows, C) for x in (history, out_cotangent, skip_cotangent)]
    vmem = pl.BlockSpec(memory_space=pltpu.VMEM)
    hbm = pl.BlockSpec(memory_space=pl.ANY)
    dma = pltpu.SemaphoreType.DMA
    V = pltpu.VMEM
    seq = jax.ShapeDtypeStruct((rows, C), BF16)
    parts = pl.pallas_call(
        functools.partial(layer_kernel, T, D),
        out_shape=[seq, seq, seq, jax.ShapeDtypeStruct((R, W), BF16)],
        in_specs=[hbm] * 8,
        out_specs=[hbm] * 3 + [vmem],
        scratch_shapes=[
            V((rows, C), BF16), V((C, W), BF16), V((C, W), BF16), V((1, W), F32),
            V((G, C), BF16), V((G, C), BF16), V((rows, C), BF16), V((rows, C), BF16),
            V((rows, C), BF16), V((rows, C), BF16), V((rows, C), BF16),
            V((rows, C), BF16), V((rows, C), BF16), V((rows, C), BF16), V((rows, C), F32),
            V((CHUNK, W), F32), V((CHUNK, G), F32), V((CHUNK, G), BF16), V((CHUNK, W), BF16),
            V((2 * C, W), F32), V((G, 2 * C), F32), V((1, W), F32),
            V((H, 2, R, G), BF16), V((H, 2, R, G), BF16), V((H, 2, 2, R, G), F32),
            V((H, R, G), BF16), V((H, R, G), BF16),
            V((H - 1, R, G), BF16), V((H - 1, R, G), BF16),
            V((S, R, lane), F32), V((S - 1, R, lane), BF16), V((S - 1, R, lane), BF16),
            V((T, R, lane), BF16),
            dma((8,)), dma((3, K)), dma((K,)), dma((K,)), dma((K,)), dma((K,)),
            dma((3,)), dma((3,)), dma((3,)), dma((3,)), dma((3, H - 1)), dma((3, H - 1)),
            dma((3, S - 1)), dma((3, S - 1)), dma((3, T - 1)), dma((3, T - 1)),
        ],
        compiler_params=pltpu.CompilerParams(
            collective_id=0, has_side_effects=True, vmem_limit_bytes=60 * 1024 * 1024
        ),
        cost_estimate=pl.CostEstimate(
            flops=rows * C * G * 36, bytes_accessed=rows * C * 12, transcendentals=rows * W
        ),
        name="gated_layer",
    )(flat[0], now_weight, past_weight, gate_bias.reshape(1, W), residual_weight, skip_weight, flat[1], flat[2])
    outs = pl.pallas_call(
        functools.partial(unpack_kernel, D),
        out_shape=[
            seq, seq, seq,
            jax.ShapeDtypeStruct((C // D, W), F32),
            jax.ShapeDtypeStruct((C // D, W), F32),
            jax.ShapeDtypeStruct((1, W // D), F32),
            jax.ShapeDtypeStruct((G // D, C), F32),
            jax.ShapeDtypeStruct((G // D, C), F32),
        ],
        in_specs=[hbm] * 3 + [vmem],
        out_specs=[hbm] * 3 + [vmem] * 5,
        scratch_shapes=[dma((3,))],
        compiler_params=pltpu.CompilerParams(vmem_limit_bytes=60 * 1024 * 1024),
        cost_estimate=pl.CostEstimate(flops=0, bytes_accessed=rows * C * 12, transcendentals=0),
        name="unpack_results",
    )(*parts)
    shape = (histories, steps, C)
    return (
        outs[0].reshape(shape), outs[1].reshape(shape), outs[2].reshape(shape),
        outs[3], outs[4], outs[5].reshape(W // D), outs[6], outs[7],
    )


def solution(mesh):
    seq = P("dp", "tm", None)
    return jax.shard_map(
        functools.partial(shards, mesh.shape["tm"], mesh.shape["dp"]),
        mesh=mesh,
        in_specs=(seq, P(), P(), P(), P(), P(), seq, seq),
        out_specs=(seq, seq, seq, P("dp", None), P("dp", None), P("dp"), P("dp", None), P("dp", None)),
        check_vma=False,
    )
```

```python
import functools

import jax
import jax.numpy as jnp
from jax import lax
from jax.experimental import pallas as pl
from jax.experimental.pallas import tpu as pltpu
from jax.sharding import PartitionSpec as P

DILATION_STEPS = 2048
CHUNK = 512
BIAS_ROWS = 16
F32 = jnp.float32
BF16 = jnp.bfloat16
MESH = pl.DeviceIdType.MESH


def dot(a, b, dims=((1,), (0,))):
    return lax.dot_general(a, b, (dims, ((), ())), preferred_element_type=F32)


NT = ((1,), (1,))
TN = ((0,), (0,))


def layer_kernel(
    T, D,
    hist_h, now_h, past_h, bias_h, res_h, skip_h, ocot_h, scot_h,
    resid_h, skipped_h, grad_in_h, packed,
    hist, now_w, past_w, bias, res_w, skip_w, ocot, scot, resid, skipped, grad_in,
    delayed, bw_send, bw_recv, gi_part, zn, dgs, gated_s, dz_s,
    acc_np, acc_rs, acc_b, a_send, a_recv, b_own, b_send, b_recv,
    tot, c_send, c_recv, d_buf,
    in_s, out_s, f_ss, f_rs, w_ss, w_rs,
    a_ss, a_rs, b_ss, b_rs, c_ss, c_rs, d_ss, d_rs,
):
    rows, C = hist.shape
    G = res_w.shape[0]
    H = D // 2
    K = rows // CHUNK
    me = lax.axis_index("tm")
    dp = lax.axis_index("dp")
    par = lax.rem(dp, 2)
    j0 = dp // 2
    up = lax.rem(me + 1, T)
    down = lax.rem(me + T - 1, T)
    has_prev = me > 0
    has_next = me < T - 1
    Rn = C // D
    Rg = G // D
    hg = Rg // 2
    W = 2 * G
    bw = W // D
    lane = W // T
    r1, r2, r3, r4 = marks(C, G, D)
    pieces = [(0, r1), (r1, r3), (r3, r4)]

    loads = [
        pltpu.make_async_copy(x, y, in_s.at[i])
        for i, (x, y) in enumerate((
            (hist_h, hist), (now_h, now_w), (ocot_h, ocot), (scot_h, scot),
            (res_h, res_w), (skip_h, skip_w), (past_h, past_w), (bias_h, bias),
        ))
    ]
    for cp in loads:
        cp.start()

    barrier = pltpu.get_barrier_semaphore()
    for o in range(1, T):
        pl.semaphore_signal(barrier, inc=1, device_id={"tm": lax.rem(me + o, T)}, device_id_type=MESH)
    for o in range(1, H):
        pl.semaphore_signal(
            barrier, inc=1, device_id={"dp": 2 * lax.rem(j0 + o, H) + par}, device_id_type=MESH
        )
    pl.semaphore_signal(barrier, inc=1, device_id={"dp": 2 * j0 + 1 - par}, device_id_type=MESH)

    @pl.when(me == 0)
    def _():
        delayed[...] = jnp.zeros_like(delayed)

    @pl.when(me == T - 1)
    def _():
        bw_recv[...] = jnp.zeros_like(bw_recv)

    acc_np[...] = jnp.zeros_like(acc_np)
    acc_rs[...] = jnp.zeros_like(acc_rs)
    acc_b[...] = jnp.zeros_like(acc_b)
    loads[0].wait()
    pl.semaphore_wait(barrier, T - 1 + H)

    def remote(src, dst, ss, rs, target):
        return pltpu.make_async_remote_copy(
            src_ref=src, dst_ref=dst, send_sem=ss, recv_sem=rs, device_id=target, device_id_type=MESH
        )

    def span(c):
        if isinstance(c, int):
            return pl.ds(c * CHUNK, CHUNK)
        return pl.ds(pl.multiple_of(c * CHUNK, CHUNK), CHUNK)

    def fwd(c):
        return remote(hist.at[span(c)], delayed.at[span(c)], f_ss.at[c], f_rs.at[c], {"tm": up})

    def bwd(c):
        return remote(bw_send.at[span(c)], bw_recv.at[span(c)], w_ss.at[c], w_rs.at[c], {"tm": down})

    def store(i, c):
        src, dst = ((resid, resid_h), (skipped, skipped_h), (grad_in, grad_in_h))[i]
        return pltpu.make_async_copy(src.at[span(c)], dst.at[span(c)], out_s.at[i, c])

    @pl.when(has_next)
    def _():
        for c in range(K):
            fwd(c).start()

    for cp in loads[1:]:
        cp.wait()

    def before(c, carry):
        s = span(c)
        dgs[s, :] = dot(ocot[s, :], res_w[...], NT) + dot(scot[s, :], skip_w[...], NT)
        return carry

    lax.fori_loop(0, K, before, 0)

    def late(c, carry):
        s = span(c)
        gated = gated_s[s, :]
        resid[s, :] = (hist[s, :].astype(F32) + dot(gated, res_w[...])).astype(BF16)
        skipped[s, :] = dot(gated, skip_w[...]).astype(BF16)
        gi_part[s, :] = ocot[s, :].astype(F32) + dot(dz_s[s, :], now_w[...], NT)
        store(0, c).start()
        store(1, c).start()
        return carry

    def core_part(c):
        s = span(c)
        zn[...] = dot(hist[s, :], now_w[...]) + bias[...]

        @pl.when(has_prev)
        def _():
            fwd(c).wait_recv()

        z = zn[...] + dot(delayed[s, :], past_w[...])
        th = jnp.tanh(z[:, :G])
        sg = 0.5 * jnp.tanh(0.5 * z[:, G:]) + 0.5
        ts = th * sg
        gated_s[s, :] = ts.astype(BF16)
        dg = dgs[s, :]
        dza = (dg * sg * (1.0 - th * th)).astype(BF16)
        dzb = (dg * ts * (1.0 - sg)).astype(BF16)
        dz = jnp.concatenate([dza, dzb], axis=1)
        dz_s[s, :] = dz
        bw_send[s, :] = dot(dz, past_w[...], NT).astype(BF16)

        @pl.when(has_prev)
        def _():
            bwd(c).start()

    def add_rs(c):
        s = span(c)
        acc_rs[:, 0:C] += dot(gated_s[s, :], ocot[s, :], TN)
        acc_rs[:, C:] += dot(gated_s[s, :], scot[s, :], TN)

    def add_now(c):
        s = span(c)
        acc_np[0:C, :] += dot(hist[s, :], dz_s[s, :], TN)
        acc_b[...] += jnp.sum(dz_s[s, :].astype(F32), axis=0, keepdims=True)

    def add_past(c):
        s = span(c)
        acc_np[C:, :] += dot(delayed[s, :], dz_s[s, :], TN)

    def step(c, carry):
        core_part(c)
        add_rs(c)
        add_now(c)
        add_past(c)
        return carry

    last = K - 1
    lax.fori_loop(0, last, step, 0)
    core_part(last)

    cores, zs, cs, ds = [], [], [], []

    def core_send(p):
        lo, hi = pieces[p]
        for j in range(H):
            a_send[j, lo:hi, :] = b_own[j, 1 - par, lo:hi, :].astype(BF16)
        cp = remote(a_send.at[:, lo:hi, :], a_recv.at[:, lo:hi, :], a_ss.at[p], a_rs.at[p],
                    {"dp": 2 * j0 + 1 - par})
        cp.start()
        cores.append(cp)

    def pair_sum(j, lo, hi):
        return b_own[j, par, lo:hi, :] + a_recv[j, lo:hi, :].astype(F32)

    def z_send(p):
        lo, hi = pieces[p]
        cores[p].wait_recv()
        for o in range(1, H):
            jt = lax.rem(j0 + o, H)
            b_send[o - 1, lo:hi, :] = pair_sum(jt, lo, hi).astype(BF16)
            cp = remote(b_send.at[o - 1, lo:hi, :], b_recv.at[o - 1, lo:hi, :],
                        b_ss.at[p, o - 1], b_rs.at[p, o - 1], {"dp": 2 * jt + par})
            cp.start()
            zs.append(cp)

    add_rs(last)
    for q in range(D):
        b_own[q // 2, q % 2, 0:r1, 0:2 * C] = acc_rs[q * Rg:q * Rg + hg, :]
        b_own[q // 2, q % 2, 0:r1, 2 * C:] = acc_rs[q * Rg + hg:(q + 1) * Rg, :]
    core_send(0)
    add_now(last)
    for q in range(D):
        blk = b_own.at[q // 2, q % 2]
        blk[r1:r2, :] = jnp.zeros((BIAS_ROWS, W), F32)
        blk[r1:r1 + 1, 0:bw] = acc_b[:, q * bw:(q + 1) * bw]
        blk[r2:r3, :] = acc_np[q * Rn:(q + 1) * Rn, :]
    core_send(1)
    z_send(0)
    add_past(last)
    for q in range(D):
        b_own[q // 2, q % 2, r3:r4, :] = acc_np[C + q * Rn:C + (q + 1) * Rn, :]
    core_send(2)
    z_send(1)
    z_send(2)
    lax.fori_loop(0, K, late, 0)

    for p, (lo, hi) in enumerate(pieces):
        total = pair_sum(j0, lo, hi)
        for o in range(1, H):
            zs[p * (H - 1) + o - 1].wait_recv()
            total = total + b_recv[o - 1, lo:hi, :].astype(F32)
        for t in range(T):
            tot[t, lo:hi, :] = total[:, t * lane:(t + 1) * lane]
        for o in range(1, T):
            t = lax.rem(me + o, T)
            c_send[o - 1, lo:hi, :] = tot[t, lo:hi, :].astype(BF16)
            cp = remote(c_send.at[o - 1, lo:hi, :], c_recv.at[o - 1, lo:hi, :],
                        c_ss.at[p, o - 1], c_rs.at[p, o - 1], {"tm": t})
            cp.start()
            cs.append(cp)

    for p, (lo, hi) in enumerate(pieces):
        mine = tot[me, lo:hi, :]
        for o in range(1, T):
            cs[p * (T - 1) + o - 1].wait_recv()
            mine = mine + c_recv[o - 1, lo:hi, :].astype(F32)
        d_buf[me, lo:hi, :] = mine.astype(BF16)
        for o in range(1, T):
            cp = remote(d_buf.at[me, lo:hi, :], d_buf.at[me, lo:hi, :], d_ss.at[p, o - 1], d_rs.at[p, o - 1],
                        {"tm": lax.rem(me + o, T)})
            cp.start()
            ds.append(cp)

    def finish(c, carry):
        s = span(c)

        @pl.when(has_next)
        def _():
            bwd(c).wait_recv()
            fwd(c).wait_send()

        grad_in[s, :] = (gi_part[s, :] + bw_recv[s, :].astype(F32)).astype(BF16)
        store(2, c).start()
        store(0, c).wait()
        store(1, c).wait()

        @pl.when(has_prev)
        def _():
            bwd(c).wait_send()

        return carry

    lax.fori_loop(0, K, finish, 0)

    for p, (lo, hi) in enumerate(pieces):
        for o in range(1, T):
            t = lax.rem(me + T - o, T)
            remote(d_buf.at[t, lo:hi, :], d_buf.at[t, lo:hi, :], d_ss.at[p, o - 1], d_rs.at[p, o - 1],
                   {"tm": lax.rem(me + o, T)}).wait_recv()
    for t in range(T):
        packed[:, t * lane:(t + 1) * lane] = d_buf[t]
    for cp in cores + zs + cs + ds:
        cp.wait_send()
    for c in range(K):
        store(2, c).wait()


def marks(C, G, D):
    r1 = G // D // 2
    r2 = r1 + BIAS_ROWS
    r3 = r2 + C // D
    return r1, r2, r3, r3 + C // D


def unpack_kernel(D, a, b, c, packed, oa, ob, oc, g_now, g_past, g_bias, g_res, g_skip, sems):
    copies = [pltpu.make_async_copy(x, y, sems.at[i]) for i, (x, y) in enumerate(((a, oa), (b, ob), (c, oc)))]
    for cp in copies:
        cp.start()
    C = a.shape[1]
    G = packed.shape[1] // 2
    r1, r2, r3, r4 = marks(C, G, D)
    g_bias[...] = packed[r1:r2, 0:2 * G // D].astype(F32)[0:1]
    for half in range(2):
        at = 2 * C * half
        g_res[half * r1:(half + 1) * r1, :] = packed[0:r1, at:at + C].astype(F32)
        g_skip[half * r1:(half + 1) * r1, :] = packed[0:r1, at + C:at + 2 * C].astype(F32)
    g_now[...] = packed[r2:r3, :].astype(F32)
    g_past[...] = packed[r3:r4, :].astype(F32)
    for cp in copies:
        cp.wait()


def shards(T, D, history, now_weight, past_weight, gate_bias, residual_weight, skip_weight,
           out_cotangent, skip_cotangent):
    histories, steps, C = history.shape
    assert steps == DILATION_STEPS
    rows = histories * steps
    G = residual_weight.shape[0]
    W = 2 * G
    K = rows // CHUNK
    H = D // 2
    R = marks(C, G, D)[3]
    lane = W // T
    flat = [x.reshape(rows, C) for x in (history, out_cotangent, skip_cotangent)]
    vmem = pl.BlockSpec(memory_space=pltpu.VMEM)
    hbm = pl.BlockSpec(memory_space=pl.ANY)
    dma = pltpu.SemaphoreType.DMA
    V = pltpu.VMEM
    seq = jax.ShapeDtypeStruct((rows, C), BF16)
    parts = pl.pallas_call(
        functools.partial(layer_kernel, T, D),
        out_shape=[seq, seq, seq, jax.ShapeDtypeStruct((R, W), BF16)],
        in_specs=[hbm] * 8,
        out_specs=[hbm] * 3 + [vmem],
        scratch_shapes=[
            V((rows, C), BF16), V((C, W), BF16), V((C, W), BF16), V((1, W), F32),
            V((G, C), BF16), V((G, C), BF16), V((rows, C), BF16), V((rows, C), BF16),
            V((rows, C), BF16), V((rows, C), BF16), V((rows, C), BF16),
            V((rows, C), BF16), V((rows, C), BF16), V((rows, C), BF16), V((rows, C), F32),
            V((CHUNK, W), F32), V((rows, G), F32), V((rows, G), BF16), V((rows, W), BF16),
            V((2 * C, W), F32), V((G, 2 * C), F32), V((1, W), F32),
            V((H, R, W), BF16), V((H, R, W), BF16), V((H, 2, R, W), F32),
            V((H - 1, R, W), BF16), V((H - 1, R, W), BF16),
            V((T, R, lane), F32), V((T - 1, R, lane), BF16), V((T - 1, R, lane), BF16),
            V((T, R, lane), BF16),
            dma((8,)), dma((3, K)), dma((K,)), dma((K,)), dma((K,)), dma((K,)),
            dma((3,)), dma((3,)), dma((3, H - 1)), dma((3, H - 1)),
            dma((3, T - 1)), dma((3, T - 1)), dma((3, T - 1)), dma((3, T - 1)),
        ],
        compiler_params=pltpu.CompilerParams(
            collective_id=0, has_side_effects=True, vmem_limit_bytes=60 * 1024 * 1024
        ),
        cost_estimate=pl.CostEstimate(
            flops=rows * C * G * 36, bytes_accessed=rows * C * 12, transcendentals=rows * W
        ),
        name="gated_layer",
    )(flat[0], now_weight, past_weight, gate_bias.reshape(1, W), residual_weight, skip_weight, flat[1], flat[2])
    outs = pl.pallas_call(
        functools.partial(unpack_kernel, D),
        out_shape=[
            seq, seq, seq,
            jax.ShapeDtypeStruct((C // D, W), F32),
            jax.ShapeDtypeStruct((C // D, W), F32),
            jax.ShapeDtypeStruct((1, W // D), F32),
            jax.ShapeDtypeStruct((G // D, C), F32),
            jax.ShapeDtypeStruct((G // D, C), F32),
        ],
        in_specs=[vmem] * 4,
        out_specs=[hbm] * 3 + [vmem] * 5,
        scratch_shapes=[dma((3,))],
        compiler_params=pltpu.CompilerParams(vmem_limit_bytes=60 * 1024 * 1024),
        cost_estimate=pl.CostEstimate(flops=0, bytes_accessed=rows * C * 12, transcendentals=0),
        name="unpack_results",
    )(*parts)
    shape = (histories, steps, C)
    return (
        outs[0].reshape(shape), outs[1].reshape(shape), outs[2].reshape(shape),
        outs[3], outs[4], outs[5].reshape(W // D), outs[6], outs[7],
    )


def solution(mesh):
    seq = P("dp", "tm", None)
    return jax.shard_map(
        functools.partial(shards, mesh.shape["tm"], mesh.shape["dp"]),
        mesh=mesh,
        in_specs=(seq, P(), P(), P(), P(), P(), seq, seq),
        out_specs=(seq, seq, seq, P("dp", None), P("dp", None), P("dp"), P("dp", None), P("dp", None)),
        check_vma=False,
    )
```

```python
import functools

import jax
import jax.numpy as jnp
from jax import lax
from jax.experimental import pallas as pl
from jax.experimental.pallas import tpu as pltpu
from jax.sharding import PartitionSpec as P

DILATION_STEPS = 2048
CHUNK = 512
BIAS_ROWS = 8
F32 = jnp.float32
BF16 = jnp.bfloat16
MESH = pl.DeviceIdType.MESH


def dot(a, b, dims=((1,), (0,))):
    return lax.dot_general(a, b, (dims, ((), ())), preferred_element_type=F32)


NT = ((1,), (1,))
TN = ((0,), (0,))


def layer_kernel(
    T, D,
    hist_h, now_h, past_h, bias_h, res_h, skip_h, ocot_h, scot_h,
    resid_h, skipped_h, grad_in_h, packed, bias_sum,
    hist, now_w, past_w, bias, res_w, skip_w, ocot, scot, resid, skipped, grad_in,
    delayed, bw_send, bw_recv, gi_part, zn, dgs, gated_s, dz_s,
    acc_np, acc_rs, acc_b, a_send, a_recv, b_own, b_send, b_recv,
    tot, c_send, c_recv, d_buf, e_own, e_core, e_send, e_recv, e_all,
    in_s, out_s, f_ss, f_rs, w_ss, w_rs,
    a_ss, a_rs, b_ss, b_rs, c_ss, c_rs, d_ss, d_rs,
    ea_ss, ea_rs, eb_ss, eb_rs, ec_ss, ec_rs,
):
    rows, C = hist.shape
    G = res_w.shape[0]
    H = D // 2
    K = rows // CHUNK
    me = lax.axis_index("tm")
    dp = lax.axis_index("dp")
    par = lax.rem(dp, 2)
    j0 = dp // 2
    up = lax.rem(me + 1, T)
    down = lax.rem(me + T - 1, T)
    has_prev = me > 0
    has_next = me < T - 1
    Rn = C // D
    Rg = G // D
    hg = Rg // 2
    W = 2 * G
    bw = W // D
    lane = W // T
    r1, r2, r3 = marks(C, G, D)
    pieces = [(0, r1), (r1, r2), (r2, r3)]

    loads = [
        pltpu.make_async_copy(x, y, in_s.at[i])
        for i, (x, y) in enumerate((
            (hist_h, hist), (now_h, now_w), (ocot_h, ocot), (scot_h, scot),
            (res_h, res_w), (skip_h, skip_w), (past_h, past_w), (bias_h, bias),
        ))
    ]
    for cp in loads:
        cp.start()

    barrier = pltpu.get_barrier_semaphore()
    for o in range(1, T):
        pl.semaphore_signal(barrier, inc=1, device_id={"tm": lax.rem(me + o, T)}, device_id_type=MESH)
    for o in range(1, H):
        pl.semaphore_signal(
            barrier, inc=1, device_id={"dp": 2 * lax.rem(j0 + o, H) + par}, device_id_type=MESH
        )
    pl.semaphore_signal(barrier, inc=1, device_id={"dp": 2 * j0 + 1 - par}, device_id_type=MESH)

    @pl.when(me == 0)
    def _():
        delayed[...] = jnp.zeros_like(delayed)

    @pl.when(me == T - 1)
    def _():
        bw_recv[...] = jnp.zeros_like(bw_recv)

    acc_np[...] = jnp.zeros_like(acc_np)
    acc_rs[...] = jnp.zeros_like(acc_rs)
    acc_b[...] = jnp.zeros_like(acc_b)
    loads[0].wait()
    pl.semaphore_wait(barrier, T - 1 + H)

    def remote(src, dst, ss, rs, target):
        return pltpu.make_async_remote_copy(
            src_ref=src, dst_ref=dst, send_sem=ss, recv_sem=rs, device_id=target, device_id_type=MESH
        )

    def span(c):
        if isinstance(c, int):
            return pl.ds(c * CHUNK, CHUNK)
        return pl.ds(pl.multiple_of(c * CHUNK, CHUNK), CHUNK)

    def fwd(c):
        return remote(hist.at[span(c)], delayed.at[span(c)], f_ss.at[c], f_rs.at[c], {"tm": up})

    def bwd(c):
        return remote(bw_send.at[span(c)], bw_recv.at[span(c)], w_ss.at[c], w_rs.at[c], {"tm": down})

    def store(i, c):
        src, dst = ((resid, resid_h), (skipped, skipped_h), (grad_in, grad_in_h))[i]
        return pltpu.make_async_copy(src.at[span(c)], dst.at[span(c)], out_s.at[i, c])

    @pl.when(has_next)
    def _():
        for c in range(K):
            fwd(c).start()

    for cp in loads[1:]:
        cp.wait()

    def before(c, carry):
        s = span(c)
        dgs[s, :] = dot(ocot[s, :], res_w[...], NT) + dot(scot[s, :], skip_w[...], NT)
        return carry

    lax.fori_loop(0, K, before, 0)

    def late(c, carry):
        s = span(c)
        gated = gated_s[s, :]
        resid[s, :] = (hist[s, :].astype(F32) + dot(gated, res_w[...])).astype(BF16)
        skipped[s, :] = dot(gated, skip_w[...]).astype(BF16)
        gi_part[s, :] = ocot[s, :].astype(F32) + dot(dz_s[s, :], now_w[...], NT)
        store(0, c).start()
        store(1, c).start()
        return carry

    def core_part(c):
        s = span(c)
        zn[...] = dot(hist[s, :], now_w[...]) + bias[...]

        @pl.when(has_prev)
        def _():
            fwd(c).wait_recv()

        z = zn[...] + dot(delayed[s, :], past_w[...])
        th = jnp.tanh(z[:, :G])
        sg = 0.5 * jnp.tanh(0.5 * z[:, G:]) + 0.5
        ts = th * sg
        gated_s[s, :] = ts.astype(BF16)
        dg = dgs[s, :]
        dza = (dg * sg * (1.0 - th * th)).astype(BF16)
        dzb = (dg * ts * (1.0 - sg)).astype(BF16)
        dz = jnp.concatenate([dza, dzb], axis=1)
        dz_s[s, :] = dz
        bw_send[s, :] = dot(dz, past_w[...], NT).astype(BF16)

        @pl.when(has_prev)
        def _():
            bwd(c).start()

    def add_rs(c):
        s = span(c)
        acc_rs[:, 0:C] += dot(gated_s[s, :], ocot[s, :], TN)
        acc_rs[:, C:] += dot(gated_s[s, :], scot[s, :], TN)

    def add_now(c):
        s = span(c)
        acc_np[0:C, :] += dot(hist[s, :], dz_s[s, :], TN)
        acc_b[...] += jnp.sum(dz_s[s, :].astype(F32), axis=0, keepdims=True)

    def add_past(c):
        s = span(c)
        acc_np[C:, :] += dot(delayed[s, :], dz_s[s, :], TN)

    def step(c, carry):
        core_part(c)
        add_rs(c)
        add_now(c)
        add_past(c)
        return carry

    last = K - 1
    lax.fori_loop(0, last, step, 0)
    core_part(last)

    cores, zs, cs, ds = [], [], [], []

    def core_send(p):
        lo, hi = pieces[p]
        for j in range(H):
            a_send[j, lo:hi, :] = b_own[j, 1 - par, lo:hi, :].astype(BF16)
        cp = remote(a_send.at[:, lo:hi, :], a_recv.at[:, lo:hi, :], a_ss.at[p], a_rs.at[p],
                    {"dp": 2 * j0 + 1 - par})
        cp.start()
        cores.append(cp)

    def pair_sum(j, lo, hi):
        return b_own[j, par, lo:hi, :] + a_recv[j, lo:hi, :].astype(F32)

    def z_send(p):
        lo, hi = pieces[p]
        cores[p].wait_recv()
        for o in range(1, H):
            jt = lax.rem(j0 + o, H)
            b_send[o - 1, lo:hi, :] = pair_sum(jt, lo, hi).astype(BF16)
            cp = remote(b_send.at[o - 1, lo:hi, :], b_recv.at[o - 1, lo:hi, :],
                        b_ss.at[p, o - 1], b_rs.at[p, o - 1], {"dp": 2 * jt + par})
            cp.start()
            zs.append(cp)

    add_rs(last)
    for q in range(D):
        b_own[q // 2, q % 2, 0:r1, 0:2 * C] = acc_rs[q * Rg:q * Rg + hg, :]
        b_own[q // 2, q % 2, 0:r1, 2 * C:] = acc_rs[q * Rg + hg:(q + 1) * Rg, :]
    core_send(0)
    add_now(last)
    for q in range(D):
        blk = b_own.at[q // 2, q % 2]
        blk[r1:r2, :] = acc_np[q * Rn:(q + 1) * Rn, :]
        e_own[q % 2, q // 2] = jnp.broadcast_to(acc_b[:, q * bw:(q + 1) * bw], (BIAS_ROWS, bw))
    core_send(1)
    ea = remote(e_own.at[1 - par], e_core, ea_ss, ea_rs, {"dp": 2 * j0 + 1 - par})
    ea.start()
    z_send(0)
    add_past(last)
    for q in range(D):
        b_own[q // 2, q % 2, r2:r3, :] = acc_np[C + q * Rn:C + (q + 1) * Rn, :]
    core_send(2)
    z_send(1)
    z_send(2)
    ea.wait_recv()
    e_core[...] += e_own[par]
    es = []
    for o in range(1, H):
        jt = lax.rem(j0 + o, H)
        cp = remote(e_core.at[jt], e_recv.at[o - 1], eb_ss.at[o - 1], eb_rs.at[o - 1], {"dp": 2 * jt + par})
        cp.start()
        es.append(cp)
    lax.fori_loop(0, K, late, 0)
    e_total = e_core[j0]
    for cp in es:
        cp.wait_recv()
    for o in range(1, H):
        e_total = e_total + e_recv[o - 1]
    e_send[...] = e_total
    e_all[me] = e_total
    ec = []
    for o in range(1, T):
        cp = remote(e_send, e_all.at[me], ec_ss.at[o - 1], ec_rs.at[o - 1], {"tm": lax.rem(me + o, T)})
        cp.start()
        ec.append(cp)

    for p, (lo, hi) in enumerate(pieces):
        total = pair_sum(j0, lo, hi)
        for o in range(1, H):
            zs[p * (H - 1) + o - 1].wait_recv()
            total = total + b_recv[o - 1, lo:hi, :].astype(F32)
        for t in range(T):
            tot[t, lo:hi, :] = total[:, t * lane:(t + 1) * lane]
        for o in range(1, T):
            t = lax.rem(me + o, T)
            c_send[o - 1, lo:hi, :] = tot[t, lo:hi, :].astype(BF16)
            cp = remote(c_send.at[o - 1, lo:hi, :], c_recv.at[o - 1, lo:hi, :],
                        c_ss.at[p, o - 1], c_rs.at[p, o - 1], {"tm": t})
            cp.start()
            cs.append(cp)

    for p, (lo, hi) in enumerate(pieces):
        mine = tot[me, lo:hi, :]
        for o in range(1, T):
            cs[p * (T - 1) + o - 1].wait_recv()
            mine = mine + c_recv[o - 1, lo:hi, :].astype(F32)
        d_buf[me, lo:hi, :] = mine.astype(BF16)
        for o in range(1, T):
            cp = remote(d_buf.at[me, lo:hi, :], d_buf.at[me, lo:hi, :], d_ss.at[p, o - 1], d_rs.at[p, o - 1],
                        {"tm": lax.rem(me + o, T)})
            cp.start()
            ds.append(cp)

    def finish(c, carry):
        s = span(c)

        @pl.when(has_next)
        def _():
            bwd(c).wait_recv()
            fwd(c).wait_send()

        grad_in[s, :] = (gi_part[s, :] + bw_recv[s, :].astype(F32)).astype(BF16)
        store(2, c).start()
        store(0, c).wait()
        store(1, c).wait()

        @pl.when(has_prev)
        def _():
            bwd(c).wait_send()

        return carry

    lax.fori_loop(0, K, finish, 0)

    for p, (lo, hi) in enumerate(pieces):
        for o in range(1, T):
            t = lax.rem(me + T - o, T)
            remote(d_buf.at[t, lo:hi, :], d_buf.at[t, lo:hi, :], d_ss.at[p, o - 1], d_rs.at[p, o - 1],
                   {"tm": lax.rem(me + o, T)}).wait_recv()
    for o in range(1, T):
        remote(e_send, e_all.at[lax.rem(me + T - o, T)], ec_ss.at[o - 1], ec_rs.at[o - 1],
               {"tm": lax.rem(me + o, T)}).wait_recv()
    e_full = e_all[0]
    for t in range(1, T):
        e_full = e_full + e_all[t]
    bias_sum[...] = e_full
    for t in range(T):
        packed[:, t * lane:(t + 1) * lane] = d_buf[t]
    for cp in [ea] + es + ec + cores + zs + cs + ds:
        cp.wait_send()
    for c in range(K):
        store(2, c).wait()


def marks(C, G, D):
    r1 = G // D // 2
    return r1, r1 + C // D, r1 + 2 * (C // D)


def unpack_kernel(D, a, b, c, packed, bias_sum, oa, ob, oc, g_now, g_past, g_bias, g_res, g_skip, held, l_s, s_s):
    rows, C = a.shape
    K = rows // CHUNK
    moves = []
    for i, (x, y) in enumerate(((a, oa), (b, ob), (c, oc))):
        for k in range(K):
            at = pl.ds(k * CHUNK, CHUNK)
            load = pltpu.make_async_copy(x.at[at], held.at[i, at], l_s.at[i, k])
            load.start()
            moves.append((load, pltpu.make_async_copy(held.at[i, at], y.at[at], s_s.at[i, k])))
    G = packed.shape[1] // 2
    r1, r2, r3 = marks(C, G, D)
    g_bias[...] = bias_sum[0:1, :]
    for half in range(2):
        at = 2 * C * half
        g_res[half * r1:(half + 1) * r1, :] = packed[0:r1, at:at + C].astype(F32)
        g_skip[half * r1:(half + 1) * r1, :] = packed[0:r1, at + C:at + 2 * C].astype(F32)
    g_now[...] = packed[r1:r2, :].astype(F32)
    g_past[...] = packed[r2:r3, :].astype(F32)
    for load, put in moves:
        load.wait()
        put.start()
    for load, put in moves:
        put.wait()


def shards(T, D, history, now_weight, past_weight, gate_bias, residual_weight, skip_weight,
           out_cotangent, skip_cotangent):
    histories, steps, C = history.shape
    assert steps == DILATION_STEPS
    rows = histories * steps
    G = residual_weight.shape[0]
    W = 2 * G
    K = rows // CHUNK
    H = D // 2
    R = marks(C, G, D)[2]
    bw = W // D
    lane = W // T
    flat = [x.reshape(rows, C) for x in (history, out_cotangent, skip_cotangent)]
    vmem = pl.BlockSpec(memory_space=pltpu.VMEM)
    hbm = pl.BlockSpec(memory_space=pl.ANY)
    dma = pltpu.SemaphoreType.DMA
    V = pltpu.VMEM
    seq = jax.ShapeDtypeStruct((rows, C), BF16)
    parts = pl.pallas_call(
        functools.partial(layer_kernel, T, D),
        out_shape=[seq, seq, seq, jax.ShapeDtypeStruct((R, W), BF16),
                   jax.ShapeDtypeStruct((BIAS_ROWS, bw), F32)],
        in_specs=[hbm] * 8,
        out_specs=[hbm] * 3 + [vmem] * 2,
        scratch_shapes=[
            V((rows, C), BF16), V((C, W), BF16), V((C, W), BF16), V((1, W), F32),
            V((G, C), BF16), V((G, C), BF16), V((rows, C), BF16), V((rows, C), BF16),
            V((rows, C), BF16), V((rows, C), BF16), V((rows, C), BF16),
            V((rows, C), BF16), V((rows, C), BF16), V((rows, C), BF16), V((rows, C), F32),
            V((CHUNK, W), F32), V((rows, G), F32), V((rows, G), BF16), V((rows, W), BF16),
            V((2 * C, W), F32), V((G, 2 * C), F32), V((1, W), F32),
            V((H, R, W), BF16), V((H, R, W), BF16), V((H, 2, R, W), F32),
            V((H - 1, R, W), BF16), V((H - 1, R, W), BF16),
            V((T, R, lane), F32), V((T - 1, R, lane), BF16), V((T - 1, R, lane), BF16),
            V((T, R, lane), BF16),
            V((2, H, BIAS_ROWS, bw), F32), V((H, BIAS_ROWS, bw), F32), V((BIAS_ROWS, bw), F32),
            V((H - 1, BIAS_ROWS, bw), F32), V((T, BIAS_ROWS, bw), F32),
            dma((8,)), dma((3, K)), dma((K,)), dma((K,)), dma((K,)), dma((K,)),
            dma((3,)), dma((3,)), dma((3, H - 1)), dma((3, H - 1)),
            dma((3, T - 1)), dma((3, T - 1)), dma((3, T - 1)), dma((3, T - 1)),
            dma, dma, dma((H - 1,)), dma((H - 1,)), dma((T - 1,)), dma((T - 1,)),
        ],
        compiler_params=pltpu.CompilerParams(
            collective_id=0, has_side_effects=True, vmem_limit_bytes=60 * 1024 * 1024
        ),
        cost_estimate=pl.CostEstimate(
            flops=rows * C * G * 36, bytes_accessed=rows * C * 12, transcendentals=rows * W
        ),
        name="gated_layer",
    )(flat[0], now_weight, past_weight, gate_bias.reshape(1, W), residual_weight, skip_weight, flat[1], flat[2])
    outs = pl.pallas_call(
        functools.partial(unpack_kernel, D),
        out_shape=[
            seq, seq, seq,
            jax.ShapeDtypeStruct((C // D, W), F32),
            jax.ShapeDtypeStruct((C // D, W), F32),
            jax.ShapeDtypeStruct((1, W // D), F32),
            jax.ShapeDtypeStruct((G // D, C), F32),
            jax.ShapeDtypeStruct((G // D, C), F32),
        ],
        in_specs=[hbm] * 3 + [vmem] * 2,
        out_specs=[hbm] * 3 + [vmem] * 5,
        scratch_shapes=[V((3, rows, C), BF16), dma((3, K)), dma((3, K))],
        compiler_params=pltpu.CompilerParams(vmem_limit_bytes=60 * 1024 * 1024),
        cost_estimate=pl.CostEstimate(flops=0, bytes_accessed=rows * C * 12, transcendentals=0),
        name="unpack_results",
    )(*parts)
    shape = (histories, steps, C)
    return (
        outs[0].reshape(shape), outs[1].reshape(shape), outs[2].reshape(shape),
        outs[3], outs[4], outs[5].reshape(W // D), outs[6], outs[7],
    )


def solution(mesh):
    seq = P("dp", "tm", None)
    return jax.shard_map(
        functools.partial(shards, mesh.shape["tm"], mesh.shape["dp"]),
        mesh=mesh,
        in_specs=(seq, P(), P(), P(), P(), P(), seq, seq),
        out_specs=(seq, seq, seq, P("dp", None), P("dp", None), P("dp"), P("dp", None), P("dp", None)),
        check_vma=False,
    )
```

```python
import functools

import jax
import jax.numpy as jnp
from jax import lax
from jax.experimental import pallas as pl
from jax.experimental.pallas import tpu as pltpu
from jax.sharding import PartitionSpec as P

DILATION_STEPS = 2048
CHUNK = 256
BIAS_ROWS = 16
F32 = jnp.float32
BF16 = jnp.bfloat16
MESH = pl.DeviceIdType.MESH


def dot(a, b, dims=((1,), (0,))):
    return lax.dot_general(a, b, (dims, ((), ())), preferred_element_type=F32)


NT = ((1,), (1,))
TN = ((0,), (0,))


def layer_kernel(
    T, D,
    hist_h, now_h, past_h, bias_h, res_h, skip_h, ocot_h, scot_h,
    resid_h, skipped_h, grad_in_h, packed,
    hist, now_w, past_w, bias, res_w, skip_w, ocot, scot, resid, skipped, grad_in,
    delayed, bw_send, bw_recv, gi_part, zn, dgs, gated_s, dz_s,
    acc_np, acc_rs, acc_b, a_send, a_recv, b_own, b_send, b_recv,
    tot, c_send, c_recv, d_buf,
    in_s, out_s, f_ss, f_rs, w_ss, w_rs,
    a_ss, a_rs, b_ss, b_rs, c_ss, c_rs, d_ss, d_rs,
):
    rows, C = hist.shape
    G = res_w.shape[0]
    H = D // 2
    K = rows // CHUNK
    me = lax.axis_index("tm")
    dp = lax.axis_index("dp")
    par = lax.rem(dp, 2)
    j0 = dp // 2
    up = lax.rem(me + 1, T)
    down = lax.rem(me + T - 1, T)
    has_prev = me > 0
    has_next = me < T - 1
    Rn = C // D
    Rg = G // D
    hg = Rg // 2
    W = 2 * G
    bw = W // D
    lane = W // T
    r1, r2, r3, r4 = marks(C, G, D)
    pieces = [(0, r1), (r1, r3), (r3, r4)]

    loads = [
        pltpu.make_async_copy(x, y, in_s.at[i])
        for i, (x, y) in enumerate((
            (hist_h, hist), (now_h, now_w), (ocot_h, ocot), (scot_h, scot),
            (res_h, res_w), (skip_h, skip_w), (past_h, past_w), (bias_h, bias),
        ))
    ]
    for cp in loads:
        cp.start()

    barrier = pltpu.get_barrier_semaphore()
    for o in range(1, T):
        pl.semaphore_signal(barrier, inc=1, device_id={"tm": lax.rem(me + o, T)}, device_id_type=MESH)
    for o in range(1, H):
        pl.semaphore_signal(
            barrier, inc=1, device_id={"dp": 2 * lax.rem(j0 + o, H) + par}, device_id_type=MESH
        )
    pl.semaphore_signal(barrier, inc=1, device_id={"dp": 2 * j0 + 1 - par}, device_id_type=MESH)

    @pl.when(me == 0)
    def _():
        delayed[...] = jnp.zeros_like(delayed)

    @pl.when(me == T - 1)
    def _():
        bw_recv[...] = jnp.zeros_like(bw_recv)

    acc_np[...] = jnp.zeros_like(acc_np)
    acc_rs[...] = jnp.zeros_like(acc_rs)
    acc_b[...] = jnp.zeros_like(acc_b)
    loads[0].wait()
    pl.semaphore_wait(barrier, T - 1 + H)

    def remote(src, dst, ss, rs, target):
        return pltpu.make_async_remote_copy(
            src_ref=src, dst_ref=dst, send_sem=ss, recv_sem=rs, device_id=target, device_id_type=MESH
        )

    def span(c):
        if isinstance(c, int):
            return pl.ds(c * CHUNK, CHUNK)
        return pl.ds(pl.multiple_of(c * CHUNK, CHUNK), CHUNK)

    def fwd(c):
        return remote(hist.at[span(c)], delayed.at[span(c)], f_ss.at[c], f_rs.at[c], {"tm": up})

    def bwd(c):
        return remote(bw_send.at[span(c)], bw_recv.at[span(c)], w_ss.at[c], w_rs.at[c], {"tm": down})

    def store(i, c):
        src, dst = ((resid, resid_h), (skipped, skipped_h), (grad_in, grad_in_h))[i]
        return pltpu.make_async_copy(src.at[span(c)], dst.at[span(c)], out_s.at[i, c])

    @pl.when(has_next)
    def _():
        for c in range(K):
            fwd(c).start()

    for cp in loads[1:]:
        cp.wait()

    def before(c, carry):
        s = span(c)
        dgs[s, :] = dot(ocot[s, :], res_w[...], NT) + dot(scot[s, :], skip_w[...], NT)
        return carry

    lax.fori_loop(0, K, before, 0)

    def late(c, carry):
        s = span(c)
        gated = gated_s[s, :]
        resid[s, :] = (hist[s, :].astype(F32) + dot(gated, res_w[...])).astype(BF16)
        skipped[s, :] = dot(gated, skip_w[...]).astype(BF16)
        gi_part[s, :] = ocot[s, :].astype(F32) + dot(dz_s[s, :], now_w[...], NT)
        store(0, c).start()
        store(1, c).start()
        return carry

    def core_part(c):
        s = span(c)
        zn[...] = dot(hist[s, :], now_w[...]) + bias[...]

        @pl.when(has_prev)
        def _():
            fwd(c).wait_recv()

        z = zn[...] + dot(delayed[s, :], past_w[...])
        th = jnp.tanh(z[:, :G])
        sg = 0.5 * jnp.tanh(0.5 * z[:, G:]) + 0.5
        ts = th * sg
        gated_s[s, :] = ts.astype(BF16)
        dg = dgs[s, :]
        dza = (dg * sg * (1.0 - th * th)).astype(BF16)
        dzb = (dg * ts * (1.0 - sg)).astype(BF16)
        dz = jnp.concatenate([dza, dzb], axis=1)
        dz_s[s, :] = dz
        bw_send[s, :] = dot(dz, past_w[...], NT).astype(BF16)

        @pl.when(has_prev)
        def _():
            bwd(c).start()

    def add_rs(c):
        s = span(c)
        acc_rs[:, 0:C] += dot(gated_s[s, :], ocot[s, :], TN)
        acc_rs[:, C:] += dot(gated_s[s, :], scot[s, :], TN)

    def add_now(c):
        s = span(c)
        acc_np[0:C, :] += dot(hist[s, :], dz_s[s, :], TN)
        acc_b[...] += jnp.sum(dz_s[s, :].astype(F32), axis=0, keepdims=True)

    def add_past(c):
        s = span(c)
        acc_np[C:, :] += dot(delayed[s, :], dz_s[s, :], TN)

    def step(c, carry):
        core_part(c)
        add_rs(c)
        add_now(c)
        add_past(c)
        return carry

    last = K - 1
    lax.fori_loop(0, last, step, 0)
    core_part(last)

    cores, zs, cs, ds = [], [], [], []

    def core_send(p):
        lo, hi = pieces[p]
        for j in range(H):
            a_send[j, lo:hi, :] = b_own[j, 1 - par, lo:hi, :].astype(BF16)
        cp = remote(a_send.at[:, lo:hi, :], a_recv.at[:, lo:hi, :], a_ss.at[p], a_rs.at[p],
                    {"dp": 2 * j0 + 1 - par})
        cp.start()
        cores.append(cp)

    def pair_sum(j, lo, hi):
        return b_own[j, par, lo:hi, :] + a_recv[j, lo:hi, :].astype(F32)

    def z_send(p):
        lo, hi = pieces[p]
        cores[p].wait_recv()
        for o in range(1, H):
            jt = lax.rem(j0 + o, H)
            b_send[o - 1, lo:hi, :] = pair_sum(jt, lo, hi).astype(BF16)
            cp = remote(b_send.at[o - 1, lo:hi, :], b_recv.at[o - 1, lo:hi, :],
                        b_ss.at[p, o - 1], b_rs.at[p, o - 1], {"dp": 2 * jt + par})
            cp.start()
            zs.append(cp)

    add_rs(last)
    for q in range(D):
        b_own[q // 2, q % 2, 0:r1, 0:2 * C] = acc_rs[q * Rg:q * Rg + hg, :]
        b_own[q // 2, q % 2, 0:r1, 2 * C:] = acc_rs[q * Rg + hg:(q + 1) * Rg, :]
    core_send(0)
    add_now(last)
    for q in range(D):
        blk = b_own.at[q // 2, q % 2]
        blk[r1:r2, :] = jnp.zeros((BIAS_ROWS, W), F32)
        blk[r1:r1 + 1, 0:bw] = acc_b[:, q * bw:(q + 1) * bw]
        blk[r2:r3, :] = acc_np[q * Rn:(q + 1) * Rn, :]
    core_send(1)
    z_send(0)
    add_past(last)
    for q in range(D):
        b_own[q // 2, q % 2, r3:r4, :] = acc_np[C + q * Rn:C + (q + 1) * Rn, :]
    core_send(2)
    z_send(1)
    z_send(2)
    lax.fori_loop(0, K, late, 0)

    for p, (lo, hi) in enumerate(pieces):
        total = pair_sum(j0, lo, hi)
        for o in range(1, H):
            zs[p * (H - 1) + o - 1].wait_recv()
            total = total + b_recv[o - 1, lo:hi, :].astype(F32)
        for t in range(T):
            tot[t, lo:hi, :] = total[:, t * lane:(t + 1) * lane]
        for o in range(1, T):
            t = lax.rem(me + o, T)
            c_send[o - 1, lo:hi, :] = tot[t, lo:hi, :].astype(BF16)
            cp = remote(c_send.at[o - 1, lo:hi, :], c_recv.at[o - 1, lo:hi, :],
                        c_ss.at[p, o - 1], c_rs.at[p, o - 1], {"tm": t})
            cp.start()
            cs.append(cp)

    for p, (lo, hi) in enumerate(pieces):
        mine = tot[me, lo:hi, :]
        for o in range(1, T):
            cs[p * (T - 1) + o - 1].wait_recv()
            mine = mine + c_recv[o - 1, lo:hi, :].astype(F32)
        d_buf[me, lo:hi, :] = mine.astype(BF16)
        for o in range(1, T):
            cp = remote(d_buf.at[me, lo:hi, :], d_buf.at[me, lo:hi, :], d_ss.at[p, o - 1], d_rs.at[p, o - 1],
                        {"tm": lax.rem(me + o, T)})
            cp.start()
            ds.append(cp)

    def finish(c, carry):
        s = span(c)

        @pl.when(has_next)
        def _():
            bwd(c).wait_recv()
            fwd(c).wait_send()

        grad_in[s, :] = (gi_part[s, :] + bw_recv[s, :].astype(F32)).astype(BF16)
        store(2, c).start()
        store(0, c).wait()
        store(1, c).wait()

        @pl.when(has_prev)
        def _():
            bwd(c).wait_send()

        return carry

    lax.fori_loop(0, K, finish, 0)

    for p, (lo, hi) in enumerate(pieces):
        for o in range(1, T):
            t = lax.rem(me + T - o, T)
            remote(d_buf.at[t, lo:hi, :], d_buf.at[t, lo:hi, :], d_ss.at[p, o - 1], d_rs.at[p, o - 1],
                   {"tm": lax.rem(me + o, T)}).wait_recv()
    for t in range(T):
        packed[:, t * lane:(t + 1) * lane] = d_buf[t]
    for cp in cores + zs + cs + ds:
        cp.wait_send()
    for c in range(K):
        store(2, c).wait()


def marks(C, G, D):
    r1 = G // D // 2
    r2 = r1 + BIAS_ROWS
    r3 = r2 + C // D
    return r1, r2, r3, r3 + C // D


def unpack_kernel(D, a, b, c, packed, oa, ob, oc, g_now, g_past, g_bias, g_res, g_skip, sems):
    copies = [pltpu.make_async_copy(x, y, sems.at[i]) for i, (x, y) in enumerate(((a, oa), (b, ob), (c, oc)))]
    for cp in copies:
        cp.start()
    C = a.shape[1]
    G = packed.shape[1] // 2
    r1, r2, r3, r4 = marks(C, G, D)
    g_bias[...] = packed[r1:r2, 0:2 * G // D].astype(F32)[0:1]
    for half in range(2):
        at = 2 * C * half
        g_res[half * r1:(half + 1) * r1, :] = packed[0:r1, at:at + C].astype(F32)
        g_skip[half * r1:(half + 1) * r1, :] = packed[0:r1, at + C:at + 2 * C].astype(F32)
    g_now[...] = packed[r2:r3, :].astype(F32)
    g_past[...] = packed[r3:r4, :].astype(F32)
    for cp in copies:
        cp.wait()


def shards(T, D, history, now_weight, past_weight, gate_bias, residual_weight, skip_weight,
           out_cotangent, skip_cotangent):
    histories, steps, C = history.shape
    assert steps == DILATION_STEPS
    rows = histories * steps
    G = residual_weight.shape[0]
    W = 2 * G
    K = rows // CHUNK
    H = D // 2
    R = marks(C, G, D)[3]
    lane = W // T
    flat = [x.reshape(rows, C) for x in (history, out_cotangent, skip_cotangent)]
    vmem = pl.BlockSpec(memory_space=pltpu.VMEM)
    hbm = pl.BlockSpec(memory_space=pl.ANY)
    dma = pltpu.SemaphoreType.DMA
    V = pltpu.VMEM
    seq = jax.ShapeDtypeStruct((rows, C), BF16)
    parts = pl.pallas_call(
        functools.partial(layer_kernel, T, D),
        out_shape=[seq, seq, seq, jax.ShapeDtypeStruct((R, W), BF16)],
        in_specs=[hbm] * 8,
        out_specs=[hbm] * 3 + [vmem],
        scratch_shapes=[
            V((rows, C), BF16), V((C, W), BF16), V((C, W), BF16), V((1, W), F32),
            V((G, C), BF16), V((G, C), BF16), V((rows, C), BF16), V((rows, C), BF16),
            V((rows, C), BF16), V((rows, C), BF16), V((rows, C), BF16),
            V((rows, C), BF16), V((rows, C), BF16), V((rows, C), BF16), V((rows, C), F32),
            V((CHUNK, W), F32), V((rows, G), F32), V((rows, G), BF16), V((rows, W), BF16),
            V((2 * C, W), F32), V((G, 2 * C), F32), V((1, W), F32),
            V((H, R, W), BF16), V((H, R, W), BF16), V((H, 2, R, W), F32),
            V((H - 1, R, W), BF16), V((H - 1, R, W), BF16),
            V((T, R, lane), F32), V((T - 1, R, lane), BF16), V((T - 1, R, lane), BF16),
            V((T, R, lane), BF16),
            dma((8,)), dma((3, K)), dma((K,)), dma((K,)), dma((K,)), dma((K,)),
            dma((3,)), dma((3,)), dma((3, H - 1)), dma((3, H - 1)),
            dma((3, T - 1)), dma((3, T - 1)), dma((3, T - 1)), dma((3, T - 1)),
        ],
        compiler_params=pltpu.CompilerParams(
            collective_id=0, has_side_effects=True, vmem_limit_bytes=60 * 1024 * 1024
        ),
        cost_estimate=pl.CostEstimate(
            flops=rows * C * G * 36, bytes_accessed=rows * C * 12, transcendentals=rows * W
        ),
        name="gated_layer",
    )(flat[0], now_weight, past_weight, gate_bias.reshape(1, W), residual_weight, skip_weight, flat[1], flat[2])
    outs = pl.pallas_call(
        functools.partial(unpack_kernel, D),
        out_shape=[
            seq, seq, seq,
            jax.ShapeDtypeStruct((C // D, W), F32),
            jax.ShapeDtypeStruct((C // D, W), F32),
            jax.ShapeDtypeStruct((1, W // D), F32),
            jax.ShapeDtypeStruct((G // D, C), F32),
            jax.ShapeDtypeStruct((G // D, C), F32),
        ],
        in_specs=[vmem] * 4,
        out_specs=[hbm] * 3 + [vmem] * 5,
        scratch_shapes=[dma((3,))],
        compiler_params=pltpu.CompilerParams(vmem_limit_bytes=60 * 1024 * 1024),
        cost_estimate=pl.CostEstimate(flops=0, bytes_accessed=rows * C * 12, transcendentals=0),
        name="unpack_results",
    )(*parts)
    shape = (histories, steps, C)
    return (
        outs[0].reshape(shape), outs[1].reshape(shape), outs[2].reshape(shape),
        outs[3], outs[4], outs[5].reshape(W // D), outs[6], outs[7],
    )


def solution(mesh):
    seq = P("dp", "tm", None)
    return jax.shard_map(
        functools.partial(shards, mesh.shape["tm"], mesh.shape["dp"]),
        mesh=mesh,
        in_specs=(seq, P(), P(), P(), P(), P(), seq, seq),
        out_specs=(seq, seq, seq, P("dp", None), P("dp", None), P("dp"), P("dp", None), P("dp", None)),
        check_vma=False,
    )
```
